32 devices in a mesh: freq: 4 (over z), row: 8 (over y, x, core).
Axes of the slice: x: 2, y: 2, z: 4, core: 2. Of those that a mesh axis runs over, the one named last changes fastest.
Arguments:
- source_field: float32 [4, 2, 2048, 2048], P('freq', None, 'row'), may hold values from -6 to 6
- receiver_field: float32 [4, 2, 2048, 2048], P('freq', None, 'row'), may hold values from -6 to 6
- slowness_store: float32 [4, 2048, 2048], P('freq', 'row'), may hold values from -0.08 to 0.08
- store_pos: int32 [4], replicated, may hold values from 0 to 3, each once
- freq_index: int32 [4], P('freq'), may hold values from 24 to 64
Outputs:
- image: float32 [2, 2048, 2048], P(None, 'row')
- source_out: float32 [4, 2, 2048, 2048], P('freq', None, 'row')
- receiver_out: float32 [4, 2, 2048, 2048], P('freq', None, 'row')
The draws below stay inside these ranges and needn't reach their ends.
Inputs may be any that keep to these rules, and one draw needn't show every extreme that they name: `store_pos`: entries are distinct.
All inputs are finite; a program needn't handle non-finite values.
Results may differ from the reference program's by a relative error of at most 0.0003.
Values sent between devices are 32-bit elements; how exact they have to be, the bound alone decides.
No kernel may reach another device: no remote copies, remote signals or barrier semaphores. Data moves between devices by JAX's collectives and lax.ppermute only.
A program may use at most 128 MiB of HBM per device.

```python
import jax
import jax.numpy as jnp
from jax import lax

NX = 2048
NY = 2048
DEPTHS = 2
NF = 4
N_FREQ = 4


def touch_ends(values, stream_key, least, largest):
    shape = values.shape
    place = [jax.random.randint(jax.random.fold_in(stream_key, axis), (), 0, shape[axis]) for axis in range(len(shape))]
    values = values.at[tuple(place)].set(least)
    longest = shape.index(max(shape))
    place[longest] = (place[longest] + 1) % shape[longest]
    return values.at[tuple(place)].set(largest)


def block_scale(own_key, extent, cuts, least, high):
    def one(axis_at, shards_of):
        heights = jax.random.uniform(jax.random.fold_in(jax.random.fold_in(own_key, 6), axis_at), (shards_of,), jnp.float32, least / len(cuts), high / len(cuts))
        return jnp.repeat(jnp.exp(heights), extent[axis_at] // shards_of).reshape((-1,) + (1,) * (len(extent) - axis_at - 1))

    gain = one(*cuts[0])
    for cut in cuts[1:]:
        gain = gain * one(*cut)
    return gain


def gaussian(key, dims, scale, most, shards=(), kind=jnp.bfloat16):
    level = block_scale(key, dims, shards, -0.22, 0.18) if shards else 1.0
    values = jax.random.normal(key, dims, jnp.float32) * scale * level
    return jnp.minimum(jnp.maximum(values, -most), most).astype(kind)


def setup_inputs(seed: int = 0) -> dict:
    streams_of = jax.random.split(jax.random.key(seed), 6)
    source_field = gaussian(streams_of[0], (NF, 2, NX, NY), 1.0, 6.0, ((0, 4), (2, 8)), jnp.float32)
    receiver_field = gaussian(streams_of[1], (NF, 2, NX, NY), 1.0, 6.0, ((0, 4), (2, 8)), jnp.float32)
    slowness_store = jnp.clip(jax.random.uniform(streams_of[2], (N_FREQ, NX, NY), jnp.float32, -0.08, 0.08) * block_scale(streams_of[2], (N_FREQ, NX, NY), ((0, 4), (1, 8)), -0.4, 0.0), -0.08, 0.08)
    store_pos = jax.random.permutation(streams_of[3], N_FREQ).astype(jnp.int32)
    freq_index = touch_ends(jax.random.randint(streams_of[4], (NF,), 24, 65), jax.random.fold_in(streams_of[4], 1), 24, 64).astype(jnp.int32)
    return dict(source_field=source_field, receiver_field=receiver_field, slowness_store=slowness_store, store_pos=store_pos, freq_index=freq_index)


depth_step = 16.0
omega_unit = 0.045

def wavenumbers(length):
    return 2.0 * jnp.pi * jnp.fft.fftfreq(length).astype(jnp.float32)

def one_step(pair, omega, orient, slowness):
    field = pair[0] + 1j * pair[1]
    spectrum = jnp.fft.fft2(field)
    kx_values = wavenumbers(NX)[:, None]
    ky_values = wavenumbers(NY)[None, :]
    phase_q = omega * omega - kx_values * kx_values - ky_values * ky_values
    travel = jnp.sqrt(jnp.maximum(phase_q, 0.0))
    decay = jnp.sqrt(jnp.maximum(-phase_q, 0.0))
    damping = jnp.exp(-depth_step * decay)
    multiplier = damping * (jnp.cos(depth_step * travel) + 1j * orient * jnp.sin(depth_step * travel))
    moved = jnp.fft.ifft2(spectrum * multiplier)
    angles = orient * omega * depth_step * slowness
    lensed = moved * (jnp.cos(angles) + 1j * jnp.sin(angles))
    return jnp.stack([jnp.real(lensed), jnp.imag(lensed)]).astype(pair.dtype)

def reference(source_field, receiver_field, slowness_store, store_pos, freq_index):
    omegas = omega_unit * freq_index.astype(jnp.float32)
    source_now = source_field
    receiver_now = receiver_field
    images = []
    for depth_index in range(DEPTHS):
        slowness = slowness_store[store_pos[depth_index]]

        def per_freq(items):
            source_pair, receiver_pair, omega = items
            source_next = one_step(source_pair, omega, -1.0, slowness)
            receiver_next = one_step(receiver_pair, omega, 1.0, slowness)
            term = source_next[0] * receiver_next[0] + source_next[1] * receiver_next[1]
            return (source_next, receiver_next, term)
        source_now, receiver_now, terms = lax.map(per_freq, (source_now, receiver_now, omegas))
        images.append(lax.optimization_barrier(jnp.sum(terms, axis=0)))
    return (jnp.stack(images), source_now, receiver_now)
```

```python
import functools

import jax
import jax.numpy as jnp
import numpy as np
from jax import lax
from jax.experimental import pallas as pl
from jax.experimental.pallas import tpu as pltpu
from jax.sharding import PartitionSpec as P

DEPTHS = 2


depth_step = 16.0
omega_unit = 0.045
lanes = 128
digits = 16
sub = 8
vmem_bytes = 60 * 1024 * 1024


def split_pair(table):
    high = table.astype(jnp.bfloat16)
    low = (table - high.astype(np.float64)).astype(jnp.bfloat16)
    return high, low


@functools.lru_cache(None)
def right_table(orient):
    index = np.arange(lanes)
    angle = orient * 2.0 * np.pi * (np.outer(index, index) % lanes) / lanes
    c, s = np.cos(angle), np.sin(angle)
    high, low = split_pair(np.block([[c, s], [-s, c]]))
    return np.concatenate([high, high, low], axis=0)


@functools.lru_cache(None)
def twiddle_table(length, orient):
    turns = np.outer(np.arange(digits), np.arange(lanes)) % length
    angle = orient * 2.0 * np.pi * turns / length
    return np.stack([np.cos(angle), np.sin(angle)]).astype(np.float32)


@functools.lru_cache(None)
def left_table(length, orient):
    index = np.arange(lanes)
    digit = np.arange(digits)
    turns = (digits * index[None, :, None] * index[None, None, :]
             + digit[:, None, None] * index[None, None, :]) % length
    if orient > 0:
        turns = np.swapaxes(turns, 1, 2)
    angle = orient * 2.0 * np.pi * turns / length
    c, s = np.cos(angle), np.sin(angle)
    full = np.concatenate([np.concatenate([c, -s], 2), np.concatenate([s, c], 2)], 1)
    high, low = split_pair(full)
    return np.concatenate([high, low], axis=2)


def four(a, b, c, d, orient):
    (ar, ai), (br, bi), (cr, ci), (dr, di) = a, b, c, d
    pr, pi = ar + cr, ai + ci
    mr, mi = ar - cr, ai - ci
    qr, qi = br + dr, bi + di
    nr, ni = br - dr, bi - di
    ir, ii = (-ni, nr) if orient > 0 else (ni, -nr)
    return [(pr + qr, pi + qi), (mr + ir, mi + ii), (pr - qr, pi - qi), (mr - ir, mi - ii)]


def turn16(value, step, orient):
    real, imag = value
    step = step % 16
    if step == 0:
        return value
    if step == 4:
        return (-imag, real) if orient > 0 else (imag, -real)
    root = float(np.sqrt(0.5))
    if step == 2:
        if orient > 0:
            return ((real - imag) * root, (real + imag) * root)
        return ((real + imag) * root, (imag - real) * root)
    if step == 6:
        if orient > 0:
            return ((real + imag) * -root, (real - imag) * root)
        return ((imag - real) * root, (real + imag) * -root)
    c = float(np.cos(2.0 * np.pi * step / 16))
    s = float(orient * np.sin(2.0 * np.pi * step / 16))
    return (real * c - imag * s, real * s + imag * c)


def sixteen(values, orient):
    inner = []
    for n2 in range(4):
        part = four(values[n2], values[4 + n2], values[8 + n2], values[12 + n2], orient)
        inner.append([turn16(part[k1], n2 * k1, orient) for k1 in range(4)])
    out = [None] * 16
    for k1 in range(4):
        part = four(inner[0][k1], inner[1][k1], inner[2][k1], inner[3][k1], orient)
        for k2 in range(4):
            out[k1 + 4 * k2] = part[k2]
    return out


def halves(value):
    high = value.astype(jnp.bfloat16)
    low = (value - high.astype(jnp.float32)).astype(jnp.bfloat16)
    return high, low


def times_right(value, table_ref):
    high, low = halves(value)
    wide = jnp.concatenate([high, low, high], axis=1)
    return jnp.dot(wide, table_ref[...], preferred_element_type=jnp.float32)


def times_left(table, value):
    high, low = halves(value)
    tall = jnp.concatenate([high, low, high], axis=0)
    wide = jnp.concatenate([table[:, :2 * lanes], table[:, :2 * lanes], table[:, 2 * lanes:]], axis=1)
    return jnp.dot(wide, tall, preferred_element_type=jnp.float32)


def product(a, b):
    return (a[0] * b[0] - a[1] * b[1], a[0] * b[1] + a[1] * b[0])


def to_last_wavenumbers(me, held, table_ref, out_refs):
    mine = out_refs[0].shape[0]
    rows = held.shape[1]
    for k, out_ref in enumerate(out_refs):
        base = (me ^ k) * mine
        done = times_right(held[pl.ds(base, mine)].reshape(mine * rows, 2 * lanes), table_ref)
        for j in range(mine):
            out_ref[j, 0] = done[j * rows:(j + 1) * rows, :lanes]
            out_ref[j, 1] = done[j * rows:(j + 1) * rows, lanes:]


def forward_last_kernel(shards, me_ref, x_ref, twid_ref, table_ref, *rest):
    outs, held = rest[:shards], rest[shards]
    rows = x_ref.shape[1]

    def one(t, carry):
        at = pl.ds(pl.multiple_of(t * sub, sub), sub)
        values = [
            (x_ref[0, at, a * lanes:(a + 1) * lanes], x_ref[1, at, a * lanes:(a + 1) * lanes])
            for a in range(digits)
        ]
        for q, value in enumerate(sixteen(values, -1)):
            if q:
                value = product(value, (twid_ref[0, q:q + 1, :], twid_ref[1, q:q + 1, :]))
            held[q, at, :lanes] = value[0]
            held[q, at, lanes:] = value[1]
        return carry

    lax.fori_loop(0, rows // sub, one, 0)
    to_last_wavenumbers(me_ref[0], held, table_ref, outs)


def smem():
    return pl.BlockSpec(memory_space=pltpu.SMEM)


def whole(table):
    return pl.BlockSpec(table.shape, lambda i: (0,) * table.ndim)


def forward_last(me, field, shards, chunk):
    _, rows, cols = field.shape
    mine = digits // shards
    twid = twiddle_table(cols, -1)
    table = right_table(-1)
    return pl.pallas_call(
        functools.partial(forward_last_kernel, shards),
        grid=(rows // chunk,),
        in_specs=[
            smem(),
            pl.BlockSpec((2, chunk, cols), lambda i: (0, i, 0)),
            whole(twid),
            whole(table),
        ],
        out_specs=[pl.BlockSpec((mine, 2, chunk, lanes), lambda i: (0, 0, i, 0))] * shards,
        out_shape=[jax.ShapeDtypeStruct((mine, 2, rows, lanes), jnp.float32)] * shards,
        scratch_shapes=[pltpu.VMEM((digits, chunk, 2 * lanes), jnp.float32)],
        compiler_params=pltpu.CompilerParams(vmem_limit_bytes=vmem_bytes),
        cost_estimate=pl.CostEstimate(
            flops=2 * 3 * rows * digits * 256 * 256, bytes_accessed=16 * rows * cols, transcendentals=0
        ),
        name="forward_last",
    )(me, field, twid, table)


def middle_kernel(sign, shards, pieces, me_ref, fwd_ref, inv_ref, mult_ref, *rest):
    ins, outs = rest[:shards], rest[shards:-2]
    held, spare = rest[-2:]
    per = digits // shards
    local = per * lanes
    me = me_ref[0]
    for k, in_ref in enumerate(ins):
        for j in range(per):
            spare[(me ^ k) * per + j] = in_ref[0, :, j * lanes:(j + 1) * lanes, :]

    def first(t, carry):
        base = pl.multiple_of(t * sub, sub)
        at = pl.ds(base, sub)
        values = [(spare[a, 0, at, :], spare[a, 1, at, :]) for a in range(digits)]
        for q, value in enumerate(sixteen(values, -1)):
            held[q, at, :] = value[0]
            held[q, pl.ds(lanes + base, sub), :] = value[1]
        return carry

    lax.fori_loop(0, lanes // sub, first, 0)

    def second(q, carry):
        spec = times_left(fwd_ref[q], held[q])
        real, imag = spec[:lanes], spec[lanes:]
        mr, mi = mult_ref[0, 0, q], mult_ref[1, 0, q]
        if sign > 0:
            moved = (real * mr - imag * mi, real * mi + imag * mr)
        else:
            moved = (real * mr + imag * mi, imag * mr - real * mi)
        held[q] = times_left(inv_ref[q], jnp.concatenate(moved, axis=0))
        return carry

    lax.fori_loop(0, digits, second, 0)

    def third(t, carry):
        base = pl.multiple_of(t * sub, sub)
        at = pl.ds(base, sub)
        values = [(held[q, at, :], held[q, pl.ds(lanes + base, sub), :]) for q in range(digits)]
        for a, value in enumerate(sixteen(values, 1)):
            spare[a, 0, at, :] = value[0]
            spare[a, 1, at, :] = value[1]
        return carry

    lax.fori_loop(0, lanes // sub, third, 0)
    start = 0
    for p, size in enumerate(pieces):
        for k in range(shards):
            out_ref = outs[p * shards + k]
            at = 0
            while at < size:
                row = start + at
                j, r = row // lanes, row % lanes
                span = min(size - at, lanes - r)
                out_ref[0, :, at:at + span, :] = spare[(me ^ k) * per + j, :, r:r + span, :]
                at += span
        start += size


def middle(me, moved, mult, sign, pieces):
    shards = len(moved)
    mine, _, rows, _ = moved[0].shape
    length = shards * rows
    fwd, inv = left_table(length, -1), left_table(length, 1)

    def block(size):
        return pl.BlockSpec((1, 2, size, lanes), lambda i: (i, 0, 0, 0))

    outs = pl.pallas_call(
        functools.partial(middle_kernel, sign, shards, pieces),
        grid=(mine,),
        in_specs=[
            smem(),
            whole(fwd),
            whole(inv),
            pl.BlockSpec((2, 1, digits, lanes, lanes), lambda i: (0, i, 0, 0, 0)),
        ] + [block(rows)] * shards,
        out_specs=[block(size) for size in pieces for _ in range(shards)],
        out_shape=[
            jax.ShapeDtypeStruct((mine, 2, size, lanes), jnp.float32) for size in pieces for _ in range(shards)
        ],
        scratch_shapes=[
            pltpu.VMEM((digits, 2 * lanes, lanes), jnp.float32),
            pltpu.VMEM((digits, 2, lanes, lanes), jnp.float32),
        ],
        compiler_params=pltpu.CompilerParams(vmem_limit_bytes=vmem_bytes),
        cost_estimate=pl.CostEstimate(
            flops=2 * 2 * 3 * rows * digits * 256 * 256,
            bytes_accessed=24 * rows * length,
            transcendentals=0,
        ),
        name="middle",
    )(me, fwd, inv, mult, *moved)
    return [outs[p * shards:(p + 1) * shards] for p in range(len(pieces))]


def space_kernel(sign, shards, onward, keep, with_image, aliased, *refs):
    refs = list(refs)
    me = refs.pop(0)[0]
    lens_ref, itwid_ref, itable_ref = refs[:3]
    del refs[:3]
    ins = refs[:shards]
    del refs[:shards]
    if with_image:
        other_ref = refs.pop(0)
    if onward:
        twid_ref, table_ref = refs[:2]
        del refs[:2]
    if aliased:
        refs.pop(0)
    held = refs.pop()
    field_ref = refs.pop(0) if keep else None
    if onward:
        outs = refs[:shards]
        del refs[:shards]
    if with_image:
        image_ref = refs.pop(0)
    mine, _, rows, _ = ins[0].shape

    for k, in_ref in enumerate(ins):
        wide = jnp.concatenate([in_ref[:, 0], in_ref[:, 1]], axis=2).reshape(mine * rows, 2 * lanes)
        held[pl.ds((me ^ k) * mine, mine)] = times_right(wide, itable_ref).reshape(mine, rows, 2 * lanes)

    def one(t, carry):
        at = pl.ds(pl.multiple_of(t * sub, sub), sub)
        values = []
        for q in range(digits):
            value = (held[q, at, :lanes], held[q, at, lanes:])
            if q:
                value = product(value, (itwid_ref[0, q:q + 1, :], itwid_ref[1, q:q + 1, :]))
            values.append(value)
        values = sixteen(values, 1)
        for a in range(digits):
            real, imag = values[a]
            col = slice(a * lanes, (a + 1) * lanes)
            c, s = lens_ref[0, at, col], lens_ref[1, at, col]
            if sign > 0:
                real, imag = real * c - imag * s, real * s + imag * c
            else:
                real, imag = real * c + imag * s, imag * c - real * s
            if keep:
                field_ref[0, at, col] = real
                field_ref[1, at, col] = imag
            if with_image:
                image_ref[at, col] = real * other_ref[0, at, col] + imag * other_ref[1, at, col]
            values[a] = (real, imag)
        if onward:
            for q, value in enumerate(sixteen(values, -1)):
                if q:
                    value = product(value, (twid_ref[0, q:q + 1, :], twid_ref[1, q:q + 1, :]))
                held[q, at, :lanes] = value[0]
                held[q, at, lanes:] = value[1]
        return carry

    lax.fori_loop(0, rows // sub, one, 0)
    if onward:
        to_last_wavenumbers(me, held, table_ref, outs)


def space(me, blocks, lens, sign, onward, other=None, keep=True, start=0, into=None, chunk=64):
    shards = len(blocks)
    mine, _, part, _ = blocks[0].shape
    _, rows, cols = lens.shape
    chunk = min(chunk, part)
    first = start // chunk
    itwid, itable = twiddle_table(cols, 1), right_table(1)
    row_spec = pl.BlockSpec((2, chunk, cols), lambda i: (0, first + i, 0))
    wave_spec = pl.BlockSpec((mine, 2, chunk, lanes), lambda i: (0, 0, i, 0))
    operands = [me, lens, itwid, itable, *blocks]
    in_specs = [smem(), row_spec, whole(itwid), whole(itable)] + [wave_spec] * shards
    if other is not None:
        operands.append(other)
        in_specs.append(row_spec)
    if onward:
        tables = [twiddle_table(cols, -1), right_table(-1)]
        operands += tables
        in_specs += [whole(table) for table in tables]
    aliases = {}
    if into is not None:
        aliases = {len(operands): 0}
        operands.append(into)
        in_specs.append(pl.BlockSpec(memory_space=pl.ANY))
    out_specs, out_shape = [], []
    if keep:
        out_specs.append(row_spec)
        out_shape.append(jax.ShapeDtypeStruct((2, rows, cols), jnp.float32))
    if onward:
        out_specs += [wave_spec] * shards
        out_shape += [jax.ShapeDtypeStruct((mine, 2, part, lanes), jnp.float32)] * shards
    if other is not None:
        out_specs.append(pl.BlockSpec((chunk, cols), lambda i: (i, 0)))
        out_shape.append(jax.ShapeDtypeStruct((part, cols), jnp.float32))
    outs = pl.pallas_call(
        functools.partial(space_kernel, sign, shards, onward, keep, other is not None, into is not None),
        grid=(part // chunk,),
        in_specs=in_specs,
        out_specs=out_specs,
        out_shape=out_shape,
        input_output_aliases=aliases,
        scratch_shapes=[pltpu.VMEM((digits, chunk, 2 * lanes), jnp.float32)],
        compiler_params=pltpu.CompilerParams(vmem_limit_bytes=vmem_bytes),
        cost_estimate=pl.CostEstimate(
            flops=(2 if onward else 1) * 2 * 3 * part * digits * 256 * 256,
            bytes_accessed=32 * part * cols,
            transcendentals=0,
        ),
        name="space",
    )(*operands)
    outs = list(outs)
    field = outs.pop(0) if keep else None
    term = outs.pop() if other is not None else None
    return field, outs, term


def wavenumber(index, length):
    signed = jnp.where(index < length // 2, index, index - length)
    return 2.0 * jnp.pi * (signed.astype(jnp.float32) / length)


def multiplier(omega, kx_index, ky_index, rows_total, cols_total):
    kx_values = wavenumber(kx_index, rows_total)
    ky_values = wavenumber(ky_index, cols_total)
    phase_q = omega * omega - (kx_values * kx_values + ky_values * ky_values)
    travel = jnp.sqrt(jnp.maximum(phase_q, 0.0))
    decay = jnp.sqrt(jnp.maximum(-phase_q, 0.0))
    damping = jnp.exp(-depth_step * decay) / (rows_total * cols_total)
    return damping * jnp.cos(depth_step * travel), damping * jnp.sin(depth_step * travel)


def swap(array, axis, mask):
    size = lax.axis_size(axis)
    return lax.ppermute(array, axis, [(d, d ^ mask) for d in range(size)])


def exchange(blocks, gates):
    if gates is not None:
        blocks = [blocks[0]] + [lax.optimization_barrier((b, g))[0] for b, g in zip(blocks[1:], gates[1:])]
    return [blocks[0]] + [swap(block, "row", k) for k, block in enumerate(blocks) if k]


def slices_of(slowness_store, store_pos):
    mine = lax.axis_index("freq")
    return [
        jnp.where(mine == store_pos[z], slowness_store[0], 0.0).astype(jnp.float32) for z in range(DEPTHS)
    ]


def on_device(source_field, receiver_field, slowness_store, store_pos, freq_index):
    omega = omega_unit * freq_index.astype(jnp.float32)[0]
    rows = source_field.shape[2]
    cols = source_field.shape[3]
    shards = lax.axis_size("row")
    n_freq = lax.axis_size("freq")
    mine = digits // shards
    rows_total = rows * shards
    me = lax.axis_index("row").astype(jnp.int32)[None]

    kept = slices_of(slowness_store, store_pos)
    slow = [lax.psum(kept[0], "freq")]
    second_kept, _ = lax.optimization_barrier((kept[1], slow[0]))
    slow.append(lax.psum(second_kept, "freq"))

    grid_shape = (mine, digits, lanes, lanes)
    kx_index = lax.broadcasted_iota(jnp.int32, grid_shape, 1) + digits * lax.broadcasted_iota(
        jnp.int32, grid_shape, 2
    )
    ky_index = (
        lax.axis_index("row") * mine
        + lax.broadcasted_iota(jnp.int32, grid_shape, 0)
        + digits * lax.broadcasted_iota(jnp.int32, grid_shape, 3)
    )
    mult = jnp.stack(multiplier(omega, kx_index, ky_index, rows_total, cols))

    spec_source = forward_last(me, source_field[0], shards, 128)
    spec_receiver = forward_last(me, receiver_field[0], shards, 128)
    images = []
    gates = None
    for z in range(DEPTHS):
        last = z == DEPTHS - 1
        moved_source = exchange(spec_source, gates)
        moved_receiver = exchange(spec_receiver, moved_source)
        (mid_source,) = middle(me, moved_source, mult, -1, (rows,))
        (mid_receiver,) = middle(me, moved_receiver, mult, 1, (rows,))
        back_source = exchange(mid_source, moved_receiver)
        back_receiver = exchange(mid_receiver, back_source)
        gates = back_receiver
        angles = depth_step * omega * slow[z]
        lens = jnp.stack([jnp.cos(angles), jnp.sin(angles)])
        source_now, spec_source, _ = space(me, back_source, lens, -1, not last)
        receiver_now, spec_receiver, term = space(
            me, back_receiver, lens, 1, not last, other=source_now, keep=last
        )
        if last:
            term, images[0] = lax.optimization_barrier((term, images[0]))
            for mask in (1, 2):
                term = term + swap(term, "freq", mask)
            images.append(term)
        else:
            images.append(lax.psum(term, "freq"))
    return jnp.stack(images), source_now[None], receiver_now[None]


def plain_step(field, mult_real, mult_imag):
    def table(length, orient):
        index = lax.broadcasted_iota(jnp.int32, (length, length), 0) * lax.broadcasted_iota(
            jnp.int32, (length, length), 1
        )
        angle = 2.0 * jnp.pi / length * (index % length).astype(jnp.float32)
        return jnp.cos(angle), orient * jnp.sin(angle)

    def along(real, imag, orient, last):
        c, s = table(real.shape[1 if last else 0], orient)
        dot = functools.partial(jnp.matmul, precision=lax.Precision.HIGHEST)
        if last:
            return dot(real, c) - dot(imag, s), dot(real, s) + dot(imag, c)
        return dot(c, real) - dot(s, imag), dot(s, real) + dot(c, imag)

    def trade(pair, split, join):
        both = lax.all_to_all(jnp.stack(pair), "row", split_axis=split, concat_axis=join, tiled=True)
        return both[0], both[1]

    real, imag = along(field[0], field[1], -1.0, True)
    real, imag = trade((real, imag), 2, 1)
    real, imag = along(real, imag, -1.0, False)
    real, imag = product((real, imag), (mult_real, mult_imag))
    real, imag = along(real, imag, 1.0, False)
    real, imag = trade((real, imag), 1, 2)
    return jnp.stack(along(real, imag, 1.0, True))


def on_device_plain(source_field, receiver_field, slowness_store, store_pos, freq_index):
    omega = omega_unit * freq_index.astype(jnp.float32)[0]
    rows = source_field.shape[2]
    cols = source_field.shape[3]
    shards = lax.axis_size("row")
    rows_total = rows * shards
    block = cols // shards
    slow = lax.psum(jnp.stack(slices_of(slowness_store, store_pos)), "freq")
    kx_index = lax.broadcasted_iota(jnp.int32, (rows_total, block), 0)
    ky_index = lax.broadcasted_iota(jnp.int32, (rows_total, block), 1) + lax.axis_index("row") * block
    mult_real, mult_imag = multiplier(omega, kx_index, ky_index, rows_total, cols)
    source_now, receiver_now = source_field[0], receiver_field[0]
    images = []
    for z in range(DEPTHS):
        angles = depth_step * omega * slow[z]
        lens_cos, lens_sin = jnp.cos(angles), jnp.sin(angles)
        source_now = plain_step(source_now, mult_real, -mult_imag)
        receiver_now = plain_step(receiver_now, mult_real, mult_imag)
        source_now = jnp.stack(product(source_now, (lens_cos, -lens_sin)))
        receiver_now = jnp.stack(product(receiver_now, (lens_cos, lens_sin)))
        images.append(lax.psum(jnp.sum(source_now * receiver_now, axis=0), "freq"))
    return jnp.stack(images), source_now[None], receiver_now[None]


def solution(mesh):
    placed = (
        P("freq", None, "row", None),
        P("freq", None, "row", None),
        P("freq", "row", None),
        P(),
        P("freq"),
    )

    def chosen(source_field, *rest):
        rows, cols = source_field.shape[2:]
        shards = lax.axis_size("row")
        length = digits * lanes
        four_freqs = lax.axis_size("freq") == 4
        fits = digits % shards == 0 and cols == length and rows * shards == length and four_freqs
        return (on_device if fits else on_device_plain)(source_field, *rest)

    return jax.shard_map(
        chosen,
        mesh=mesh,
        in_specs=placed,
        out_specs=(
            P(None, "row", None),
            P("freq", None, "row", None),
            P("freq", None, "row", None),
        ),
        check_vma=False,
    )
```

```python
import functools
import math

import jax
import jax.numpy as jnp
import numpy as np
from jax import lax
from jax.experimental import pallas as pl
from jax.experimental.pallas import tpu as pltpu
from jax.sharding import PartitionSpec as P

DEPTHS = 2


depth_step = 16.0
omega_unit = 0.045
lanes = 128
digits = 16
sub = 8
vmem_bytes = 60 * 1024 * 1024


def split_pair(table):
    high = table.astype(jnp.bfloat16)
    low = (table - high.astype(np.float64)).astype(jnp.bfloat16)
    return high, low


@functools.lru_cache(None)
def right_table(orient):
    index = np.arange(lanes)
    angle = orient * 2.0 * np.pi * (np.outer(index, index) % lanes) / lanes
    c, s = np.cos(angle), np.sin(angle)
    high, low = split_pair(np.block([[c, s], [-s, c]]))
    return np.concatenate([high, high, low], axis=0)


@functools.lru_cache(None)
def twiddle_table(length, orient):
    turns = np.outer(np.arange(digits), np.arange(lanes)) % length
    angle = orient * 2.0 * np.pi * turns / length
    return np.stack([np.cos(angle), np.sin(angle)]).astype(np.float32)


@functools.lru_cache(None)
def left_table(length, orient):
    index = np.arange(lanes)
    digit = np.arange(digits)
    turns = (digits * index[None, :, None] * index[None, None, :]
             + digit[:, None, None] * index[None, None, :]) % length
    if orient > 0:
        turns = np.swapaxes(turns, 1, 2)
    angle = orient * 2.0 * np.pi * turns / length
    c, s = np.cos(angle), np.sin(angle)
    full = np.concatenate([np.concatenate([c, -s], 2), np.concatenate([s, c], 2)], 1)
    high, low = split_pair(full)
    return np.concatenate([high, low], axis=2)


def four(a, b, c, d, orient):
    (ar, ai), (br, bi), (cr, ci), (dr, di) = a, b, c, d
    pr, pi = ar + cr, ai + ci
    mr, mi = ar - cr, ai - ci
    qr, qi = br + dr, bi + di
    nr, ni = br - dr, bi - di
    ir, ii = (-ni, nr) if orient > 0 else (ni, -nr)
    return [(pr + qr, pi + qi), (mr + ir, mi + ii), (pr - qr, pi - qi), (mr - ir, mi - ii)]


def turn16(value, step, orient):
    real, imag = value
    step = step % 16
    if step == 0:
        return value
    if step == 4:
        return (-imag, real) if orient > 0 else (imag, -real)
    root = float(np.sqrt(0.5))
    if step == 2:
        if orient > 0:
            return ((real - imag) * root, (real + imag) * root)
        return ((real + imag) * root, (imag - real) * root)
    if step == 6:
        if orient > 0:
            return ((real + imag) * -root, (real - imag) * root)
        return ((imag - real) * root, (real + imag) * -root)
    c = float(np.cos(2.0 * np.pi * step / 16))
    s = float(orient * np.sin(2.0 * np.pi * step / 16))
    return (real * c - imag * s, real * s + imag * c)


def sixteen(values, orient):
    inner = []
    for n2 in range(4):
        part = four(values[n2], values[4 + n2], values[8 + n2], values[12 + n2], orient)
        inner.append([turn16(part[k1], n2 * k1, orient) for k1 in range(4)])
    out = [None] * 16
    for k1 in range(4):
        part = four(inner[0][k1], inner[1][k1], inner[2][k1], inner[3][k1], orient)
        for k2 in range(4):
            out[k1 + 4 * k2] = part[k2]
    return out


def halves(value):
    high = value.astype(jnp.bfloat16)
    low = (value - high.astype(jnp.float32)).astype(jnp.bfloat16)
    return high, low


def times_right(value, table_ref):
    high, low = halves(value)
    wide = jnp.concatenate([high, low, high], axis=1)
    return jnp.dot(wide, table_ref[...], preferred_element_type=jnp.float32)


def times_left(table, value):
    high, low = halves(value)
    tall = jnp.concatenate([high, low, high], axis=0)
    wide = jnp.concatenate([table[:, :2 * lanes], table[:, :2 * lanes], table[:, 2 * lanes:]], axis=1)
    return jnp.dot(wide, tall, preferred_element_type=jnp.float32)


sine_terms = [(-1.0) ** n / math.factorial(2 * n + 1) for n in range(6)]
cosine_terms = [(-1.0) ** n / math.factorial(2 * n) for n in range(7)]
pi_high = float(np.float32(np.pi).astype(jnp.bfloat16))
pi_low = float(np.pi - pi_high)


def series(terms, square):
    total = square * terms[-1] + terms[-2]
    for term in reversed(terms[:-2]):
        total = total * square + term
    return total


def cos_sin(angle):
    turns = jnp.floor(angle * (1.0 / np.pi) + 0.5)
    rest = (angle - turns * pi_high) - turns * pi_low
    flip = 1.0 - 2.0 * (turns - 2.0 * jnp.floor(turns * 0.5))
    square = rest * rest
    return flip * series(cosine_terms, square), flip * rest * series(sine_terms, square)


def product(a, b):
    return (a[0] * b[0] - a[1] * b[1], a[0] * b[1] + a[1] * b[0])


shards = 8


def block_shapes(rows):
    return [jax.ShapeDtypeStruct((2, 2, rows, lanes), jnp.float32)] * shards


def block_specs(rows):
    return [pl.BlockSpec((2, 2, rows, lanes), lambda i: (0, 0, i, 0))] * shards


def swap(array, axis, mask):
    size = lax.axis_size(axis)
    return lax.ppermute(array, axis, [(d, d ^ mask) for d in range(size)])


def after(value, *others):
    return lax.optimization_barrier((value, *others))[0]


def exchange(blocks, gate=None):
    if gate is not None:
        blocks = [blocks[0]] + [after(block, seen) for block, seen in zip(blocks[1:], gate[1:])]
    return [blocks[0]] + [swap(block, "row", k) for k, block in enumerate(blocks) if k]


def to_last_wavenumbers(me, held, table_ref, outs):
    rows = held.shape[1]
    for k in range(shards):
        done = times_right(held[pl.ds((me ^ k) * 2, 2)].reshape(2 * rows, 2 * lanes), table_ref)
        for j in range(2):
            for c in range(2):
                outs[k][j, c] = done[j * rows:(j + 1) * rows, c * lanes:(c + 1) * lanes]


def forward_last_kernel(me_ref, x_ref, twid_ref, table_ref, *rest):
    outs, held = rest[:-1], rest[-1]
    rows = x_ref.shape[1]

    def one(t, carry):
        at = pl.ds(pl.multiple_of(t * sub, sub), sub)
        values = [
            (x_ref[0, at, a * lanes:(a + 1) * lanes], x_ref[1, at, a * lanes:(a + 1) * lanes])
            for a in range(digits)
        ]
        for q, value in enumerate(sixteen(values, -1)):
            if q:
                value = product(value, (twid_ref[0, q:q + 1, :], twid_ref[1, q:q + 1, :]))
            held[q, at, :lanes] = value[0]
            held[q, at, lanes:] = value[1]
        return carry

    lax.fori_loop(0, rows // sub, one, 0)
    to_last_wavenumbers(me_ref[0], held, table_ref, outs)


def light():
    return pl.CostEstimate(flops=1000, bytes_accessed=1000, transcendentals=0)


def smem():
    return pl.BlockSpec(memory_space=pltpu.SMEM)


def whole(table):
    return pl.BlockSpec(table.shape, lambda i: (0,) * table.ndim)


def params():
    return pltpu.CompilerParams(vmem_limit_bytes=vmem_bytes)


def forward_last(me, field, chunk):
    _, rows, cols = field.shape
    twid = twiddle_table(cols, -1)
    table = right_table(-1)
    return pl.pallas_call(
        forward_last_kernel,
        grid=(rows // chunk,),
        in_specs=[
            smem(),
            pl.BlockSpec((2, chunk, cols), lambda i: (0, i, 0)),
            whole(twid),
            whole(table),
        ],
        out_specs=block_specs(chunk),
        out_shape=block_shapes(rows),
        scratch_shapes=[pltpu.VMEM((digits, chunk, 2 * lanes), jnp.float32)],
        compiler_params=params(),
        cost_estimate=light(),
        name="forward_last",
    )(me, field, twid, table)


def middle_kernel(sign, pieces, me_ref, fwd_ref, inv_ref, mr_ref, mi_ref, *rest):
    ins, (held, spare) = rest[:shards], rest[-2:]
    outs = rest[-2 - shards * max(len(pieces), 1):-2]
    me = me_ref[0]
    for j in range(2):
        col = slice(j * lanes, (j + 1) * lanes)
        for k in range(shards):
            for n in range(2):
                spare[(me ^ k) * 2 + n, :, :, col] = ins[k][j, :, n * lanes:(n + 1) * lanes, :]

    def first(t, carry):
        base = pl.multiple_of(t // 2 * sub, sub)
        col = pl.ds(pl.multiple_of(t % 2 * lanes, lanes), lanes)
        at = pl.ds(base, sub)
        values = [(spare[a, 0, at, col], spare[a, 1, at, col]) for a in range(digits)]
        for q, value in enumerate(sixteen(values, -1)):
            held[q, at, col] = value[0]
            held[q, pl.ds(lanes + base, sub), col] = value[1]
        return carry

    lax.fori_loop(0, 2 * lanes // sub, first, 0)

    def second(q, carry):
        spec = times_left(fwd_ref[q], held[q])
        real, imag = spec[:lanes], spec[lanes:]
        mr, mi = mr_ref[q], mi_ref[q]
        if sign > 0:
            moved = (real * mr - imag * mi, real * mi + imag * mr)
        else:
            moved = (real * mr + imag * mi, imag * mr - real * mi)
        held[q] = times_left(inv_ref[q], jnp.concatenate(moved, axis=0))
        return carry

    lax.fori_loop(0, digits, second, 0)

    def third(t, carry):
        base = pl.multiple_of(t // 2 * sub, sub)
        col = pl.ds(pl.multiple_of(t % 2 * lanes, lanes), lanes)
        at = pl.ds(base, sub)
        values = [(held[q, at, col], held[q, pl.ds(lanes + base, sub), col]) for q in range(digits)]
        for a, value in enumerate(sixteen(values, 1)):
            spare[a, 0, at, col] = value[0]
            spare[a, 1, at, col] = value[1]
        return carry

    lax.fori_loop(0, 2 * lanes // sub, third, 0)
    start = 0
    for p, size in enumerate(pieces or (outs[0].shape[2],)):
        at = 0
        while at < size:
            n, r = (start + at) // lanes, (start + at) % lanes
            span = min(size - at, lanes - r)
            for k in range(shards):
                for j in range(2):
                    col = slice(j * lanes, (j + 1) * lanes)
                    value = spare[(me ^ k) * 2 + n, :, r:r + span, col]
                    if pieces:
                        outs[p * shards + k][0, j, :, at:at + span] = value
                    else:
                        outs[k][j, :, at:at + span] = value
            at += span
        start += size


def middle(me, blocks, mult, sign, pieces=(), into=None):
    rows = blocks[0].shape[2]
    length = shards * rows
    fwd, inv = left_table(length, -1), left_table(length, 1)
    operands = [me, fwd, inv, *mult, *blocks]
    in_specs = [smem(), whole(fwd), whole(inv), whole(mult[0]), whole(mult[1])] + block_specs(rows)
    aliases = {}
    out_specs, out_shape = block_specs(rows), block_shapes(rows)
    if pieces:
        out_specs, out_shape = [], []
        for p, (size, fields, place) in enumerate(pieces):
            for k in range(shards):
                out_specs.append(pl.BlockSpec((1, 2, 2, size, lanes), lambda i, place=place: (place, 0, 0, 0, 0)))
                out_shape.append(jax.ShapeDtypeStruct((fields, 2, 2, size, lanes), jnp.float32))
                if place:
                    aliases[len(operands)] = p * shards + k
                    operands.append(into[p][k])
                    in_specs.append(pl.BlockSpec(memory_space=pl.ANY))
    outs = pl.pallas_call(
        functools.partial(middle_kernel, sign, tuple(size for size, _, _ in pieces)),
        grid=(1,),
        in_specs=in_specs,
        out_specs=out_specs,
        out_shape=out_shape,
        input_output_aliases=aliases,
        scratch_shapes=[
            pltpu.VMEM((digits, 2 * lanes, 2 * lanes), jnp.float32),
            pltpu.VMEM((digits, 2, lanes, 2 * lanes), jnp.float32),
        ],
        compiler_params=params(),
        cost_estimate=light(),
        name="middle",
    )(*operands)
    return [outs[p * shards:(p + 1) * shards] for p in range(len(pieces))] if pieces else outs


def space_kernel(sign, onward, keep, image, aliased, *refs):
    refs = list(refs)
    me = refs.pop(0)[0]
    if image == "halves":
        bit = refs.pop(0)[0]
    scale_ref, slow_ref, itwid_ref, itable_ref = refs[:4]
    del refs[:4]
    scale = scale_ref[0]
    ins = refs[:shards]
    del refs[:shards]
    if image:
        other_ref = refs.pop(0)
    if onward:
        twid_ref, table_ref = refs[:2]
        del refs[:2]
    if aliased:
        refs.pop(0)
    field_ref = refs.pop(0) if keep else None
    if onward:
        outs = refs[:shards]
        del refs[:shards]
    if image == "halves":
        mine_ref, theirs_ref, held, image_ref = refs
    elif image:
        image_ref, held = refs
    else:
        (held,) = refs
    rows = held.shape[1]

    for k in range(shards):
        block = ins[k][0] if len(ins[k].shape) == 5 else ins[k][...]
        wide = [jnp.concatenate([block[j, 0], block[j, 1]], axis=1) for j in range(2)]
        done = times_right(jnp.concatenate(wide, axis=0), itable_ref)
        held[pl.ds((me ^ k) * 2, 2)] = done.reshape(2, rows, 2 * lanes)

    def one(t, carry):
        at = pl.ds(pl.multiple_of(t * sub, sub), sub)
        values = []
        for q in range(digits):
            value = (held[q, at, :lanes], held[q, at, lanes:])
            if q:
                value = product(value, (itwid_ref[0, q:q + 1, :], itwid_ref[1, q:q + 1, :]))
            values.append(value)
        values = sixteen(values, 1)
        for a in range(digits):
            real, imag = values[a]
            col = slice(a * lanes, (a + 1) * lanes)
            c, s = cos_sin(scale * slow_ref[0, at, col])
            if sign > 0:
                real, imag = real * c - imag * s, real * s + imag * c
            else:
                real, imag = real * c + imag * s, imag * c - real * s
            if keep:
                field_ref[0, at, col] = real
                field_ref[1, at, col] = imag
            if image:
                image_ref[at, col] = real * other_ref[0, at, col] + imag * other_ref[1, at, col]
            values[a] = (real, imag)
        if onward:
            for q, value in enumerate(sixteen(values, -1)):
                if q:
                    value = product(value, (twid_ref[0, q:q + 1, :], twid_ref[1, q:q + 1, :]))
                held[q, at, :lanes] = value[0]
                held[q, at, lanes:] = value[1]
        return carry

    lax.fori_loop(0, rows // sub, one, 0)
    if image == "halves":
        half = rows // 2
        mine_ref[...] = image_ref[pl.ds(pl.multiple_of(bit * half, sub), half), :]
        theirs_ref[...] = image_ref[pl.ds(pl.multiple_of((1 - bit) * half, sub), half), :]
    if onward:
        to_last_wavenumbers(me, held, table_ref, outs)


def space(me, blocks, scale, slow, z, sign, onward, other=None, keep=True, start=0, into=None, bit=None, chunk=128):
    _, rows, cols = slow.shape
    if isinstance(blocks, tuple):
        blocks, place = blocks
        part = blocks[0].shape[3]
        chunk = min(chunk, part)
        specs = [pl.BlockSpec((1, 2, 2, chunk, lanes), lambda i: (place, 0, 0, i, 0))] * shards
    else:
        part = blocks[0].shape[2]
        specs = block_specs(chunk)
    first = start // chunk
    image = None if other is None else "whole" if bit is None else "halves"
    itwid, itable = twiddle_table(cols, 1), right_table(1)
    field_spec = pl.BlockSpec((2, chunk, cols), lambda i: (0, first + i, 0))
    slow_spec = pl.BlockSpec((1, chunk, cols), lambda i: (z, first + i, 0))
    operands, in_specs = [me], [smem()]
    if image == "halves":
        operands.append(bit)
        in_specs.append(smem())
    operands += [scale, slow, itwid, itable]
    in_specs += [smem(), slow_spec, whole(itwid), whole(itable)]
    operands += blocks
    in_specs += specs
    if image:
        operands.append(other)
        in_specs.append(field_spec)
    if onward:
        tables = [twiddle_table(cols, -1), right_table(-1)]
        operands += tables
        in_specs += [whole(table) for table in tables]
    aliases = {}
    if into is not None:
        aliases = {len(operands): 0}
        operands.append(into)
        in_specs.append(pl.BlockSpec(memory_space=pl.ANY))
    out_specs, out_shape = [], []
    scratch = [pltpu.VMEM((digits, chunk, 2 * lanes), jnp.float32)]
    if keep:
        out_specs.append(field_spec)
        out_shape.append(jax.ShapeDtypeStruct((2, rows, cols), jnp.float32))
    if onward:
        out_specs += block_specs(chunk)
        out_shape += block_shapes(part)
    if image == "whole":
        out_specs.append(pl.BlockSpec((chunk, cols), lambda i: (i, 0)))
        out_shape.append(jax.ShapeDtypeStruct((part, cols), jnp.float32))
    elif image:
        out_specs += [pl.BlockSpec((chunk // 2, cols), lambda i: (i, 0))] * 2
        out_shape += [jax.ShapeDtypeStruct((part // 2, cols), jnp.float32)] * 2
        scratch.append(pltpu.VMEM((chunk, cols), jnp.float32))
    outs = pl.pallas_call(
        functools.partial(space_kernel, sign, onward, keep, image, into is not None),
        grid=(part // chunk,),
        in_specs=in_specs,
        out_specs=out_specs,
        out_shape=out_shape,
        input_output_aliases=aliases,
        scratch_shapes=scratch,
        compiler_params=params(),
        cost_estimate=light(),
        name="space",
    )(*operands)
    outs = list(outs)
    field = outs.pop(0) if keep else None
    onward_blocks = outs[:shards] if onward else None
    if image == "halves":
        term = outs[-2:]
    else:
        term = outs[-1] if image else None
    return field, onward_blocks, term


def put_kernel(halved, bit_ref, *refs):
    refs, out_ref = list(refs[:-2]), refs[-1]
    bit = bit_ref[0]
    at = 0
    for two in halved:
        size = refs[0].shape[0]
        if two:
            mine, theirs = refs.pop(0), refs.pop(0)
            out_ref[0, pl.ds(pl.multiple_of(at + bit * size, sub), size), :] = mine[...]
            out_ref[0, pl.ds(pl.multiple_of(at + (1 - bit) * size, sub), size), :] = theirs[...]
            at += 2 * size
        else:
            out_ref[0, at:at + size, :] = refs.pop(0)[...]
            at += size


def put(image, z, bit, sums):
    flat = []
    for value in sums:
        flat += list(value) if isinstance(value, tuple) else [value]
    return pl.pallas_call(
        functools.partial(put_kernel, [isinstance(value, tuple) for value in sums]),
        grid=(1,),
        in_specs=[smem()] + [whole(v) for v in flat] + [pl.BlockSpec(memory_space=pl.ANY)],
        out_specs=pl.BlockSpec((1,) + image.shape[1:], lambda i: (z, 0, 0)),
        out_shape=jax.ShapeDtypeStruct(image.shape, jnp.float32),
        input_output_aliases={1 + len(flat): 0},
        compiler_params=params(),
        cost_estimate=light(),
        name="put",
    )(bit, *flat, image)


def wavenumber(index, length):
    signed = jnp.where(index < length // 2, index, index - length)
    return 2.0 * jnp.pi * (signed.astype(jnp.float32) / length)


def multiplier(omega, kx_index, ky_index, rows_total, cols_total):
    kx_values = wavenumber(kx_index, rows_total)
    ky_values = wavenumber(ky_index, cols_total)
    phase_q = omega * omega - (kx_values * kx_values + ky_values * ky_values)
    travel = jnp.sqrt(jnp.maximum(phase_q, 0.0))
    decay = jnp.sqrt(jnp.maximum(-phase_q, 0.0))
    damping = jnp.exp(-depth_step * decay) / (rows_total * cols_total)
    return damping * jnp.cos(depth_step * travel), damping * jnp.sin(depth_step * travel)


def slices_of(slowness_store, store_pos):
    mine = lax.axis_index("freq")
    return jnp.stack([
        jnp.where(mine == store_pos[z], slowness_store[0], 0.0).astype(jnp.float32) for z in range(DEPTHS)
    ])


def on_device(source_field, receiver_field, slowness_store, store_pos, freq_index):
    omega = omega_unit * freq_index.astype(jnp.float32)[0]
    rows = source_field.shape[2]
    cols = source_field.shape[3]
    rows_total = rows * 8
    me = lax.axis_index("row").astype(jnp.int32)[None]
    bit = lax.axis_index("freq").astype(jnp.int32)[None] & 1

    grid_shape = (digits, lanes, 2 * lanes)
    kx_index = lax.broadcasted_iota(jnp.int32, grid_shape, 0) + digits * lax.broadcasted_iota(
        jnp.int32, grid_shape, 1
    )
    column = lax.broadcasted_iota(jnp.int32, grid_shape, 2)
    ky_index = lax.axis_index("row") * 2 + column // lanes + digits * (column % lanes)
    def behind(*arrays):
        return after(me, *arrays)

    spec_source = forward_last(me, source_field[0], 128)
    moved_source = exchange(spec_source)
    kept = slices_of(after(slowness_store, moved_source[1]), store_pos)
    slow = lax.psum(kept, "freq")
    mult = multiplier(after(omega, *moved_source), kx_index, ky_index, rows_total, cols)

    scale = (depth_step * omega)[None]

    spec_receiver = forward_last(behind(kept), receiver_field[0], 128)
    moved_receiver = exchange(spec_receiver, moved_source)
    mid_source = middle(behind(spec_receiver[0]), moved_source, mult, -1)
    mid_receiver = middle(behind(mid_source[0]), moved_receiver, mult, 1)
    back_source = exchange(mid_source, moved_receiver)
    back_receiver = exchange(mid_receiver, back_source)
    source_now, spec_source, _ = space(behind(mid_receiver[0]), back_source, scale, slow, 0, -1, True)
    _, spec_receiver, term = space(me, back_receiver, scale, slow, 0, 1, True, other=source_now, keep=False)
    first_image = lax.psum(term, "freq")

    moved_source = exchange(spec_source, back_receiver)
    moved_receiver = exchange(spec_receiver, moved_source)
    sizes = (rows // 2, rows // 4, rows // 4)
    mid_source = middle(
        behind(spec_receiver[0]), moved_source, mult, -1,
        tuple((size, min(n, 1) + 1, 0) for n, size in enumerate(sizes)),
    )
    image = put(jnp.zeros((DEPTHS, rows, cols), jnp.float32), 0, bit, [first_image])
    first_source = exchange(mid_source[0], moved_receiver)
    mid_receiver = middle(
        me, moved_receiver, mult, 1, tuple((size, min(n, 1) + 1, min(n, 1)) for n, size in enumerate(sizes)),
        mid_source,
    )
    source_now = receiver_now = None
    sums = []
    start = 0
    seen = first_source
    for n, size in enumerate(sizes):
        moved = exchange(mid_receiver[n], seen)
        seen = moved
        back_source, back_receiver = ((moved, 0), (moved, 1)) if n else ((first_source, 0), (moved, 0))
        source_now, _, _ = space(
            behind(mid_receiver[-1][0], image) if n == 0 else me, back_source, scale, slow, 1, -1, False, start=start, into=source_now
        )
        receiver_now, _, term = space(
            me, back_receiver, scale, slow, 1, 1, False, other=source_now, start=start, into=receiver_now, bit=bit
        )
        start += size
        mine, theirs = term
        mine = mine + swap(theirs, "freq", 1)
        mine = mine + swap(mine, "freq", 2)
        sums.append((mine, swap(mine, "freq", 1)))
    return put(image, 1, bit, sums), source_now[None], receiver_now[None]


def plain_step(field, mult_real, mult_imag):
    def table(length, orient):
        index = lax.broadcasted_iota(jnp.int32, (length, length), 0) * lax.broadcasted_iota(
            jnp.int32, (length, length), 1
        )
        angle = 2.0 * jnp.pi / length * (index % length).astype(jnp.float32)
        return jnp.cos(angle), orient * jnp.sin(angle)

    def along(real, imag, orient, last):
        c, s = table(real.shape[1 if last else 0], orient)
        dot = functools.partial(jnp.matmul, precision=lax.Precision.HIGHEST)
        if last:
            return dot(real, c) - dot(imag, s), dot(real, s) + dot(imag, c)
        return dot(c, real) - dot(s, imag), dot(s, real) + dot(c, imag)

    def trade(pair, split, join):
        both = lax.all_to_all(jnp.stack(pair), "row", split_axis=split, concat_axis=join, tiled=True)
        return both[0], both[1]

    real, imag = along(field[0], field[1], -1.0, True)
    real, imag = trade((real, imag), 2, 1)
    real, imag = along(real, imag, -1.0, False)
    real, imag = product((real, imag), (mult_real, mult_imag))
    real, imag = along(real, imag, 1.0, False)
    real, imag = trade((real, imag), 1, 2)
    return jnp.stack(along(real, imag, 1.0, True))


def on_device_plain(source_field, receiver_field, slowness_store, store_pos, freq_index):
    omega = omega_unit * freq_index.astype(jnp.float32)[0]
    rows = source_field.shape[2]
    cols = source_field.shape[3]
    shards = lax.axis_size("row")
    rows_total = rows * shards
    block = cols // shards
    slow = lax.psum(slices_of(slowness_store, store_pos), "freq")
    kx_index = lax.broadcasted_iota(jnp.int32, (rows_total, block), 0)
    ky_index = lax.broadcasted_iota(jnp.int32, (rows_total, block), 1) + lax.axis_index("row") * block
    mult_real, mult_imag = multiplier(omega, kx_index, ky_index, rows_total, cols)
    source_now, receiver_now = source_field[0], receiver_field[0]
    images = []
    for z in range(DEPTHS):
        angles = depth_step * omega * slow[z]
        lens_cos, lens_sin = jnp.cos(angles), jnp.sin(angles)
        source_now = plain_step(source_now, mult_real, -mult_imag)
        receiver_now = plain_step(receiver_now, mult_real, mult_imag)
        source_now = jnp.stack(product(source_now, (lens_cos, -lens_sin)))
        receiver_now = jnp.stack(product(receiver_now, (lens_cos, lens_sin)))
        images.append(lax.psum(jnp.sum(source_now * receiver_now, axis=0), "freq"))
    return jnp.stack(images), source_now[None], receiver_now[None]


def solution(mesh):
    placed = (
        P("freq", None, "row", None),
        P("freq", None, "row", None),
        P("freq", "row", None),
        P(),
        P("freq"),
    )

    def chosen(source_field, *rest):
        rows, cols = source_field.shape[2:]
        split = lax.axis_size("row")
        length = digits * lanes
        fits = split == shards and lax.axis_size("freq") == 4 and cols == length and rows * split == length
        return (on_device if fits else on_device_plain)(source_field, *rest)

    return jax.shard_map(
        chosen,
        mesh=mesh,
        in_specs=placed,
        out_specs=(
            P(None, "row", None),
            P("freq", None, "row", None),
            P("freq", None, "row", None),
        ),
        check_vma=False,
    )
```

```python
import functools
import math

import jax
import jax.numpy as jnp
import numpy as np
from jax import lax
from jax.experimental import pallas as pl
from jax.experimental.pallas import tpu as pltpu
from jax.sharding import PartitionSpec as P

DEPTHS = 2


depth_step = 16.0
omega_unit = 0.045
lanes = 128
digits = 16
sub = 8
vmem_bytes = 60 * 1024 * 1024


def split_pair(table):
    high = table.astype(jnp.bfloat16)
    low = (table - high.astype(np.float64)).astype(jnp.bfloat16)
    return high, low


@functools.lru_cache(None)
def right_table(orient):
    index = np.arange(lanes)
    angle = orient * 2.0 * np.pi * (np.outer(index, index) % lanes) / lanes
    c, s = np.cos(angle), np.sin(angle)
    high, low = split_pair(np.block([[c, s], [-s, c]]))
    return np.concatenate([high, high, low], axis=0)


@functools.lru_cache(None)
def twiddle_table(length, orient):
    turns = np.outer(np.arange(digits), np.arange(lanes)) % length
    angle = orient * 2.0 * np.pi * turns / length
    return np.stack([np.cos(angle), np.sin(angle)]).astype(np.float32)


@functools.lru_cache(None)
def left_table(length, orient):
    index = np.arange(lanes)
    digit = np.arange(digits)
    turns = (digits * index[None, :, None] * index[None, None, :]
             + digit[:, None, None] * index[None, None, :]) % length
    if orient > 0:
        turns = np.swapaxes(turns, 1, 2)
    angle = orient * 2.0 * np.pi * turns / length
    c, s = np.cos(angle), np.sin(angle)
    full = np.concatenate([np.concatenate([c, -s], 2), np.concatenate([s, c], 2)], 1)
    high, low = split_pair(full)
    return np.concatenate([high, low], axis=2)


def four(a, b, c, d, orient):
    (ar, ai), (br, bi), (cr, ci), (dr, di) = a, b, c, d
    pr, pi = ar + cr, ai + ci
    mr, mi = ar - cr, ai - ci
    qr, qi = br + dr, bi + di
    nr, ni = br - dr, bi - di
    ir, ii = (-ni, nr) if orient > 0 else (ni, -nr)
    return [(pr + qr, pi + qi), (mr + ir, mi + ii), (pr - qr, pi - qi), (mr - ir, mi - ii)]


def turn16(value, step, orient):
    real, imag = value
    step = step % 16
    if step == 0:
        return value
    if step == 4:
        return (-imag, real) if orient > 0 else (imag, -real)
    root = float(np.sqrt(0.5))
    if step == 2:
        if orient > 0:
            return ((real - imag) * root, (real + imag) * root)
        return ((real + imag) * root, (imag - real) * root)
    if step == 6:
        if orient > 0:
            return ((real + imag) * -root, (real - imag) * root)
        return ((imag - real) * root, (real + imag) * -root)
    c = float(np.cos(2.0 * np.pi * step / 16))
    s = float(orient * np.sin(2.0 * np.pi * step / 16))
    return (real * c - imag * s, real * s + imag * c)


def sixteen(values, orient):
    inner = []
    for n2 in range(4):
        part = four(values[n2], values[4 + n2], values[8 + n2], values[12 + n2], orient)
        inner.append([turn16(part[k1], n2 * k1, orient) for k1 in range(4)])
    out = [None] * 16
    for k1 in range(4):
        part = four(inner[0][k1], inner[1][k1], inner[2][k1], inner[3][k1], orient)
        for k2 in range(4):
            out[k1 + 4 * k2] = part[k2]
    return out


def halves(value):
    high = value.astype(jnp.bfloat16)
    low = (value - high.astype(jnp.float32)).astype(jnp.bfloat16)
    return high, low


def times_right(value, table_ref):
    high, low = halves(value)
    wide = jnp.concatenate([high, low, high], axis=1)
    return jnp.dot(wide, table_ref[...], preferred_element_type=jnp.float32)


def times_left(table, value):
    high, low = halves(value)
    tall = jnp.concatenate([high, low, high], axis=0)
    wide = jnp.concatenate([table[:, :2 * lanes], table[:, :2 * lanes], table[:, 2 * lanes:]], axis=1)
    return jnp.dot(wide, tall, preferred_element_type=jnp.float32)


sine_terms = [(-1.0) ** n / math.factorial(2 * n + 1) for n in range(6)]
cosine_terms = [(-1.0) ** n / math.factorial(2 * n) for n in range(7)]
pi_high = float(np.float32(np.pi).astype(jnp.bfloat16))
pi_low = float(np.pi - pi_high)


def series(terms, square):
    total = square * terms[-1] + terms[-2]
    for term in reversed(terms[:-2]):
        total = total * square + term
    return total


def cos_sin(angle):
    turns = jnp.floor(angle * (1.0 / np.pi) + 0.5)
    rest = (angle - turns * pi_high) - turns * pi_low
    flip = 1.0 - 2.0 * (turns - 2.0 * jnp.floor(turns * 0.5))
    square = rest * rest
    return flip * series(cosine_terms, square), flip * rest * series(sine_terms, square)


def product(a, b):
    return (a[0] * b[0] - a[1] * b[1], a[0] * b[1] + a[1] * b[0])


shards = 8


def block_shapes(rows):
    return [jax.ShapeDtypeStruct((2, 2, rows, lanes), jnp.float32)] * shards


def block_specs(rows):
    return [pl.BlockSpec((2, 2, rows, lanes), lambda i, *_: (0, 0, i, 0))] * shards


def swap(array, axis, mask):
    size = lax.axis_size(axis)
    return lax.ppermute(array, axis, [(d, d ^ mask) for d in range(size)])


def after(value, *others):
    return lax.optimization_barrier((value, *others))[0]


def exchange(blocks, gate=None):
    if gate is not None:
        blocks = [blocks[0]] + [after(block, seen) for block, seen in zip(blocks[1:], gate[1:])]
    return [blocks[0]] + [swap(block, "row", k) for k, block in enumerate(blocks) if k]


def to_last_wavenumbers(me, held, table_ref, outs):
    rows = held.shape[1]
    for k in range(shards):
        done = times_right(held[pl.ds((me ^ k) * 2, 2)].reshape(2 * rows, 2 * lanes), table_ref)
        for j in range(2):
            for c in range(2):
                outs[k][j, c] = done[j * rows:(j + 1) * rows, c * lanes:(c + 1) * lanes]


def forward_last_kernel(me_ref, x_ref, twid_ref, table_ref, *rest):
    outs, held = rest[:-1], rest[-1]
    rows = x_ref.shape[1]

    def one(t, carry):
        at = pl.ds(pl.multiple_of(t * sub, sub), sub)
        values = [
            (x_ref[0, at, a * lanes:(a + 1) * lanes], x_ref[1, at, a * lanes:(a + 1) * lanes])
            for a in range(digits)
        ]
        for q, value in enumerate(sixteen(values, -1)):
            if q:
                value = product(value, (twid_ref[0, q:q + 1, :], twid_ref[1, q:q + 1, :]))
            held[q, at, :lanes] = value[0]
            held[q, at, lanes:] = value[1]
        return carry

    lax.fori_loop(0, rows // sub, one, 0)
    to_last_wavenumbers(me_ref[0], held, table_ref, outs)


def light():
    return pl.CostEstimate(flops=1000, bytes_accessed=1000, transcendentals=0)


def smem():
    return pl.BlockSpec(memory_space=pltpu.SMEM)


def whole(table):
    return pl.BlockSpec(table.shape, lambda i, *_: (0,) * table.ndim)


def params():
    return pltpu.CompilerParams(vmem_limit_bytes=vmem_bytes)


def forward_last(me, field, chunk):
    _, rows, cols = field.shape
    twid = twiddle_table(cols, -1)
    table = right_table(-1)
    return pl.pallas_call(
        forward_last_kernel,
        grid=(rows // chunk,),
        in_specs=[
            smem(),
            pl.BlockSpec((2, chunk, cols), lambda i: (0, i, 0)),
            whole(twid),
            whole(table),
        ],
        out_specs=block_specs(chunk),
        out_shape=block_shapes(rows),
        scratch_shapes=[pltpu.VMEM((digits, chunk, 2 * lanes), jnp.float32)],
        compiler_params=params(),
        cost_estimate=light(),
        name="forward_last",
    )(me, field, twid, table)


def middle_kernel(sign, pieces, me_ref, fwd_ref, inv_ref, mr_ref, mi_ref, *rest):
    ins, (held, spare) = rest[:shards], rest[-2:]
    outs = rest[-2 - shards * max(len(pieces), 1):-2]
    me = me_ref[0]
    step, steps = pl.program_id(0), digits // fwd_ref.shape[0]

    @pl.when(step == 0)
    def _():
        along_first(me, ins, held, spare)

    def second(n, carry):
        q = step * fwd_ref.shape[0] + n
        spec = times_left(fwd_ref[n], held[q])
        real, imag = spec[:lanes], spec[lanes:]
        mr, mi = mr_ref[n], mi_ref[n]
        if sign > 0:
            moved = (real * mr - imag * mi, real * mi + imag * mr)
        else:
            moved = (real * mr + imag * mi, imag * mr - real * mi)
        held[q] = times_left(inv_ref[n], jnp.concatenate(moved, axis=0))
        return carry

    lax.fori_loop(0, fwd_ref.shape[0], second, 0)

    @pl.when(step == steps - 1)
    def _():
        along_last(me, pieces, outs, held, spare)


def along_first(me, ins, held, spare):
    for j in range(2):
        col = slice(j * lanes, (j + 1) * lanes)
        for k in range(shards):
            for n in range(2):
                spare[(me ^ k) * 2 + n, :, :, col] = ins[k][j, :, n * lanes:(n + 1) * lanes, :]

    def first(t, carry):
        base = pl.multiple_of(t // 2 * sub, sub)
        col = pl.ds(pl.multiple_of(t % 2 * lanes, lanes), lanes)
        at = pl.ds(base, sub)
        values = [(spare[a, 0, at, col], spare[a, 1, at, col]) for a in range(digits)]
        for q, value in enumerate(sixteen(values, -1)):
            held[q, at, col] = value[0]
            held[q, pl.ds(lanes + base, sub), col] = value[1]
        return carry

    lax.fori_loop(0, 2 * lanes // sub, first, 0)


def along_last(me, pieces, outs, held, spare):
    def third(t, carry):
        base = pl.multiple_of(t // 2 * sub, sub)
        col = pl.ds(pl.multiple_of(t % 2 * lanes, lanes), lanes)
        at = pl.ds(base, sub)
        values = [(held[q, at, col], held[q, pl.ds(lanes + base, sub), col]) for q in range(digits)]
        for a, value in enumerate(sixteen(values, 1)):
            spare[a, 0, at, col] = value[0]
            spare[a, 1, at, col] = value[1]
        return carry

    lax.fori_loop(0, 2 * lanes // sub, third, 0)
    start = 0
    for p, size in enumerate(pieces or (outs[0].shape[2],)):
        at = 0
        while at < size:
            n, r = (start + at) // lanes, (start + at) % lanes
            span = min(size - at, lanes - r)
            for k in range(shards):
                for j in range(2):
                    col = slice(j * lanes, (j + 1) * lanes)
                    value = spare[(me ^ k) * 2 + n, :, r:r + span, col]
                    if pieces:
                        outs[p * shards + k][0, j, :, at:at + span] = value
                    else:
                        outs[k][j, :, at:at + span] = value
            at += span
        start += size


def middle(me, blocks, mult, sign, pieces=(), into=None):
    rows = blocks[0].shape[2]
    length = shards * rows
    fwd, inv = left_table(length, -1), left_table(length, 1)
    operands = [me, fwd, inv, *mult, *blocks]
    steps = 4

    def by_step(table):
        return pl.BlockSpec((digits // steps,) + table.shape[1:], lambda i: (i, 0, 0))

    in_specs = [smem(), by_step(fwd), by_step(inv), by_step(mult[0]), by_step(mult[1])]
    in_specs += [pl.BlockSpec((2, 2, rows, lanes), lambda i: (0, 0, 0, 0))] * shards
    aliases = {}
    out_specs = [pl.BlockSpec((2, 2, rows, lanes), lambda i: (0, 0, 0, 0))] * shards
    out_shape = block_shapes(rows)
    if pieces:
        out_specs, out_shape = [], []
        for p, (size, fields, place) in enumerate(pieces):
            for k in range(shards):
                out_specs.append(pl.BlockSpec((1, 2, 2, size, lanes), lambda i, place=place: (place, 0, 0, 0, 0)))
                out_shape.append(jax.ShapeDtypeStruct((fields, 2, 2, size, lanes), jnp.float32))
                if place:
                    aliases[len(operands)] = p * shards + k
                    operands.append(into[p][k])
                    in_specs.append(pl.BlockSpec(memory_space=pl.ANY))
    outs = pl.pallas_call(
        functools.partial(middle_kernel, sign, tuple(size for size, _, _ in pieces)),
        grid=(steps,),
        in_specs=in_specs,
        out_specs=out_specs,
        out_shape=out_shape,
        input_output_aliases=aliases,
        scratch_shapes=[
            pltpu.VMEM((digits, 2 * lanes, 2 * lanes), jnp.float32),
            pltpu.VMEM((digits, 2, lanes, 2 * lanes), jnp.float32),
        ],
        compiler_params=params(),
        cost_estimate=light(),
        name="middle",
    )(*operands)
    return [outs[p * shards:(p + 1) * shards] for p in range(len(pieces))] if pieces else outs


def space_kernel(sign, onward, keep, image, aliased, *refs):
    refs = list(refs[1:])
    me = refs.pop(0)[0]
    if image == "halves":
        bit = refs.pop(0)[0]
    scale_ref, slow_ref, itwid_ref, itable_ref = refs[:4]
    del refs[:4]
    scale = scale_ref[0]
    ins = refs[:shards]
    del refs[:shards]
    if image:
        other_ref = refs.pop(0)
    if onward:
        twid_ref, table_ref = refs[:2]
        del refs[:2]
    if aliased:
        refs.pop(0)
    field_ref = refs.pop(0) if keep else None
    if onward:
        outs = refs[:shards]
        del refs[:shards]
    if image == "halves":
        mine_ref, theirs_ref, held, image_ref = refs
    elif image:
        image_ref, held = refs
    else:
        (held,) = refs
    rows = held.shape[1]

    for k in range(shards):
        block = ins[k][0] if len(ins[k].shape) == 5 else ins[k][...]
        wide = [jnp.concatenate([block[j, 0], block[j, 1]], axis=1) for j in range(2)]
        done = times_right(jnp.concatenate(wide, axis=0), itable_ref)
        held[pl.ds((me ^ k) * 2, 2)] = done.reshape(2, rows, 2 * lanes)

    def one(t, carry):
        at = pl.ds(pl.multiple_of(t * sub, sub), sub)
        values = []
        for q in range(digits):
            value = (held[q, at, :lanes], held[q, at, lanes:])
            if q:
                value = product(value, (itwid_ref[0, q:q + 1, :], itwid_ref[1, q:q + 1, :]))
            values.append(value)
        values = sixteen(values, 1)
        for a in range(digits):
            real, imag = values[a]
            col = slice(a * lanes, (a + 1) * lanes)
            c, s = cos_sin(scale * slow_ref[0, at, col])
            if sign > 0:
                real, imag = real * c - imag * s, real * s + imag * c
            else:
                real, imag = real * c + imag * s, imag * c - real * s
            if keep:
                field_ref[0, at, col] = real
                field_ref[1, at, col] = imag
            if image:
                image_ref[at, col] = real * other_ref[0, at, col] + imag * other_ref[1, at, col]
            values[a] = (real, imag)
        if onward:
            for q, value in enumerate(sixteen(values, -1)):
                if q:
                    value = product(value, (twid_ref[0, q:q + 1, :], twid_ref[1, q:q + 1, :]))
                held[q, at, :lanes] = value[0]
                held[q, at, lanes:] = value[1]
        return carry

    lax.fori_loop(0, rows // sub, one, 0)
    if image == "halves":
        half = rows // 2
        mine_ref[...] = image_ref[pl.ds(pl.multiple_of(bit * half, sub), half), :]
        theirs_ref[...] = image_ref[pl.ds(pl.multiple_of((1 - bit) * half, sub), half), :]
    if onward:
        to_last_wavenumbers(me, held, table_ref, outs)


def space(me, blocks, scale, slow, store_pos, z, sign, onward, other=None, keep=True, start=0, into=None, bit=None, chunk=128):
    _, rows, cols = slow.shape
    if isinstance(blocks, tuple):
        blocks, place = blocks
        part = blocks[0].shape[3]
        chunk = min(chunk, part)
        specs = [pl.BlockSpec((1, 2, 2, chunk, lanes), lambda i, *_: (place, 0, 0, i, 0))] * shards
    else:
        part = blocks[0].shape[2]
        specs = block_specs(chunk)
    first = start // chunk
    image = None if other is None else "whole" if bit is None else "halves"
    itwid, itable = twiddle_table(cols, 1), right_table(1)
    field_spec = pl.BlockSpec((2, chunk, cols), lambda i, *_: (0, first + i, 0))
    slow_spec = pl.BlockSpec((1, chunk, cols), lambda i, at: (at[z], first + i, 0))
    operands, in_specs = [store_pos, me], [smem()]
    if image == "halves":
        operands.append(bit)
        in_specs.append(smem())
    operands += [scale, slow, itwid, itable]
    in_specs += [smem(), slow_spec, whole(itwid), whole(itable)]
    operands += blocks
    in_specs += specs
    if image:
        operands.append(other)
        in_specs.append(field_spec)
    if onward:
        tables = [twiddle_table(cols, -1), right_table(-1)]
        operands += tables
        in_specs += [whole(table) for table in tables]
    aliases = {}
    if into is not None:
        aliases = {len(operands): 0}
        operands.append(into)
        in_specs.append(pl.BlockSpec(memory_space=pl.ANY))
    out_specs, out_shape = [], []
    scratch = [pltpu.VMEM((digits, chunk, 2 * lanes), jnp.float32)]
    if keep:
        out_specs.append(field_spec)
        out_shape.append(jax.ShapeDtypeStruct((2, rows, cols), jnp.float32))
    if onward:
        out_specs += block_specs(chunk)
        out_shape += block_shapes(part)
    if image == "whole":
        out_specs.append(pl.BlockSpec((chunk, cols), lambda i, *_: (i, 0)))
        out_shape.append(jax.ShapeDtypeStruct((part, cols), jnp.float32))
    elif image:
        out_specs += [pl.BlockSpec((chunk // 2, cols), lambda i, *_: (i, 0))] * 2
        out_shape += [jax.ShapeDtypeStruct((part // 2, cols), jnp.float32)] * 2
        scratch.append(pltpu.VMEM((chunk, cols), jnp.float32))
    outs = pl.pallas_call(
        functools.partial(space_kernel, sign, onward, keep, image, into is not None),
        grid_spec=pltpu.PrefetchScalarGridSpec(
            num_scalar_prefetch=1,
            grid=(part // chunk,),
            in_specs=in_specs,
            out_specs=out_specs,
            scratch_shapes=scratch,
        ),
        out_shape=out_shape,
        input_output_aliases=aliases,
        compiler_params=params(),
        cost_estimate=light(),
        name="space",
    )(*operands)
    outs = list(outs)
    field = outs.pop(0) if keep else None
    onward_blocks = outs[:shards] if onward else None
    if image == "halves":
        term = outs[-2:]
    else:
        term = outs[-1] if image else None
    return field, onward_blocks, term


def put_kernel(halved, bit_ref, *refs):
    refs, out_ref = list(refs), refs[-1]
    bit = bit_ref[0]
    at = 0
    for two in halved:
        size = refs[0].shape[0]
        if two:
            mine, theirs = refs.pop(0), refs.pop(0)
            out_ref[0, pl.ds(pl.multiple_of(at + bit * size, sub), size), :] = mine[...]
            out_ref[0, pl.ds(pl.multiple_of(at + (1 - bit) * size, sub), size), :] = theirs[...]
            at += 2 * size
        else:
            out_ref[0, at:at + size, :] = refs.pop(0)[...]
            at += size


def put(image, z, bit, sums):
    flat = []
    for value in sums:
        flat += list(value) if isinstance(value, tuple) else [value]
    in_specs = [smem()] + [whole(v) for v in flat]
    operands = [bit, *flat]
    aliases = {}
    if isinstance(image, tuple):
        shape = image
    else:
        shape = image.shape
        aliases = {len(operands): 0}
        operands.append(image)
        in_specs.append(pl.BlockSpec(memory_space=pl.ANY))
    return pl.pallas_call(
        functools.partial(put_kernel, [isinstance(value, tuple) for value in sums]),
        grid=(1,),
        in_specs=in_specs,
        out_specs=pl.BlockSpec((1,) + shape[1:], lambda i: (z, 0, 0)),
        out_shape=jax.ShapeDtypeStruct(shape, jnp.float32),
        input_output_aliases=aliases,
        compiler_params=params(),
        cost_estimate=light(),
        name="put",
    )(*operands)


def wavenumber(index, length):
    signed = jnp.where(index < length // 2, index, index - length)
    return 2.0 * jnp.pi * (signed.astype(jnp.float32) / length)


def multiplier(omega, kx_index, ky_index, rows_total, cols_total):
    kx_values = wavenumber(kx_index, rows_total)
    ky_values = wavenumber(ky_index, cols_total)
    phase_q = omega * omega - (kx_values * kx_values + ky_values * ky_values)
    travel = jnp.sqrt(jnp.maximum(phase_q, 0.0))
    decay = jnp.sqrt(jnp.maximum(-phase_q, 0.0))
    damping = jnp.exp(-depth_step * decay) / (rows_total * cols_total)
    return damping * jnp.cos(depth_step * travel), damping * jnp.sin(depth_step * travel)


def on_device(source_field, receiver_field, slowness_store, store_pos, freq_index):
    omega = omega_unit * freq_index.astype(jnp.float32)[0]
    rows = source_field.shape[2]
    cols = source_field.shape[3]
    rows_total = rows * 8
    me = lax.axis_index("row").astype(jnp.int32)[None]
    bit = lax.axis_index("freq").astype(jnp.int32)[None] & 1

    grid_shape = (digits, lanes, 2 * lanes)
    kx_index = lax.broadcasted_iota(jnp.int32, grid_shape, 0) + digits * lax.broadcasted_iota(
        jnp.int32, grid_shape, 1
    )
    column = lax.broadcasted_iota(jnp.int32, grid_shape, 2)
    ky_index = lax.axis_index("row") * 2 + column // lanes + digits * (column % lanes)
    def behind(*arrays):
        return after(me, *arrays)

    spec_source = forward_last(me, source_field[0], 128)
    moved_source = exchange(spec_source)
    slow = lax.all_gather(slowness_store, "freq", axis=0, tiled=True)
    mult = multiplier(after(omega, *moved_source), kx_index, ky_index, rows_total, cols)

    scale = (depth_step * omega)[None]

    spec_receiver = forward_last(behind(moved_source[1]), receiver_field[0], 128)
    moved_receiver = exchange(spec_receiver, moved_source)
    mid_source = middle(behind(spec_receiver[0]), moved_source, mult, -1)
    mid_receiver = middle(behind(mid_source[0]), moved_receiver, mult, 1)
    back_source = exchange(mid_source, moved_receiver)
    back_receiver = exchange(mid_receiver, back_source)
    source_now, spec_source, _ = space(behind(mid_receiver[0]), back_source, scale, slow, store_pos, 0, -1, True)
    _, spec_receiver, term = space(me, back_receiver, scale, slow, store_pos, 0, 1, True, other=source_now, keep=False)
    first_image = lax.psum(term, "freq")

    moved_source = exchange(spec_source, back_receiver)
    moved_receiver = exchange(spec_receiver, moved_source)
    sizes = (rows // 2, rows // 4, rows // 4)
    mid_source = middle(
        behind(spec_receiver[0]), moved_source, mult, -1,
        tuple((size, min(n, 1) + 1, 0) for n, size in enumerate(sizes)),
    )
    image = put((DEPTHS, rows, cols), 0, bit, [first_image])
    mid_receiver = middle(
        me, moved_receiver, mult, 1, tuple((size, min(n, 1) + 1, min(n, 1)) for n, size in enumerate(sizes)),
        mid_source,
    )
    late = [after(block, mid_receiver[0][0]) for block in mid_source[0][1:3]]
    first_source = exchange([mid_source[0][0], *late, *mid_source[0][3:]], moved_receiver)
    source_now = receiver_now = None
    sums = []
    marks = []
    start = 0
    seen = first_source
    for n, size in enumerate(sizes):
        blocks = mid_receiver[n]
        if n == 2:
            late = [after(block, mark) for block, mark in zip(blocks[1:3], marks[2:0:-1])]
            blocks = [blocks[0], *late, *[after(block, marks[0]) for block in blocks[3:]]]
        moved = exchange(blocks, seen)
        seen = moved
        back_source, back_receiver = ((moved, 0), (moved, 1)) if n else ((first_source, 0), (moved, 0))
        source_now, _, _ = space(
            behind(mid_receiver[-1][0], image) if n == 0 else me, back_source, scale, slow, store_pos, 1, -1, False, start=start, into=source_now
        )
        receiver_now, _, term = space(
            me, back_receiver, scale, slow, store_pos, 1, 1, False, other=source_now, start=start, into=receiver_now,
            bit=bit if n else None,
        )
        start += size
        if n == 0:
            sums.append(lax.psum(after(term, image), "freq"))
            marks.append(term)
            continue
        mine, theirs = term
        marks.append(theirs)
        mine = mine + swap(theirs, "freq", 1)
        marks.append(mine)
        mine = mine + swap(mine, "freq", 2)
        sums.append((mine, swap(mine, "freq", 1)))
    return put(image, 1, bit, sums), source_now[None], receiver_now[None]


def plain_step(field, mult_real, mult_imag):
    def table(length, orient):
        index = lax.broadcasted_iota(jnp.int32, (length, length), 0) * lax.broadcasted_iota(
            jnp.int32, (length, length), 1
        )
        angle = 2.0 * jnp.pi / length * (index % length).astype(jnp.float32)
        return jnp.cos(angle), orient * jnp.sin(angle)

    def along(real, imag, orient, last):
        c, s = table(real.shape[1 if last else 0], orient)
        dot = functools.partial(jnp.matmul, precision=lax.Precision.HIGHEST)
        if last:
            return dot(real, c) - dot(imag, s), dot(real, s) + dot(imag, c)
        return dot(c, real) - dot(s, imag), dot(s, real) + dot(c, imag)

    def trade(pair, split, join):
        both = lax.all_to_all(jnp.stack(pair), "row", split_axis=split, concat_axis=join, tiled=True)
        return both[0], both[1]

    real, imag = along(field[0], field[1], -1.0, True)
    real, imag = trade((real, imag), 2, 1)
    real, imag = along(real, imag, -1.0, False)
    real, imag = product((real, imag), (mult_real, mult_imag))
    real, imag = along(real, imag, 1.0, False)
    real, imag = trade((real, imag), 1, 2)
    return jnp.stack(along(real, imag, 1.0, True))


def on_device_plain(source_field, receiver_field, slowness_store, store_pos, freq_index):
    omega = omega_unit * freq_index.astype(jnp.float32)[0]
    rows = source_field.shape[2]
    cols = source_field.shape[3]
    shards = lax.axis_size("row")
    rows_total = rows * shards
    block = cols // shards
    slow = lax.all_gather(slowness_store, "freq", axis=0, tiled=True)
    kx_index = lax.broadcasted_iota(jnp.int32, (rows_total, block), 0)
    ky_index = lax.broadcasted_iota(jnp.int32, (rows_total, block), 1) + lax.axis_index("row") * block
    mult_real, mult_imag = multiplier(omega, kx_index, ky_index, rows_total, cols)
    source_now, receiver_now = source_field[0], receiver_field[0]
    images = []
    for z in range(DEPTHS):
        angles = depth_step * omega * slow[store_pos[z]]
        lens_cos, lens_sin = jnp.cos(angles), jnp.sin(angles)
        source_now = plain_step(source_now, mult_real, -mult_imag)
        receiver_now = plain_step(receiver_now, mult_real, mult_imag)
        source_now = jnp.stack(product(source_now, (lens_cos, -lens_sin)))
        receiver_now = jnp.stack(product(receiver_now, (lens_cos, lens_sin)))
        images.append(lax.psum(jnp.sum(source_now * receiver_now, axis=0), "freq"))
    return jnp.stack(images), source_now[None], receiver_now[None]


def solution(mesh):
    placed = (
        P("freq", None, "row", None),
        P("freq", None, "row", None),
        P("freq", "row", None),
        P(),
        P("freq"),
    )

    def chosen(source_field, *rest):
        rows, cols = source_field.shape[2:]
        split = lax.axis_size("row")
        length = digits * lanes
        fits = split == shards and lax.axis_size("freq") == 4 and cols == length and rows * split == length
        return (on_device if fits else on_device_plain)(source_field, *rest)

    return jax.shard_map(
        chosen,
        mesh=mesh,
        in_specs=placed,
        out_specs=(
            P(None, "row", None),
            P("freq", None, "row", None),
            P("freq", None, "row", None),
        ),
        check_vma=False,
    )
```

```python
import functools
import math

import jax
import jax.numpy as jnp
import numpy as np
from jax import lax
from jax.experimental import pallas as pl
from jax.experimental.pallas import tpu as pltpu
from jax.sharding import PartitionSpec as P

DEPTHS = 2


depth_step = 16.0
omega_unit = 0.045
lanes = 128
digits = 16
sub = 8
vmem_bytes = 60 * 1024 * 1024


def split_pair(table):
    high = table.astype(jnp.bfloat16)
    low = (table - high.astype(np.float64)).astype(jnp.bfloat16)
    return high, low


@functools.lru_cache(None)
def right_table(orient):
    index = np.arange(lanes)
    angle = orient * 2.0 * np.pi * (np.outer(index, index) % lanes) / lanes
    c, s = np.cos(angle), np.sin(angle)
    high, low = split_pair(np.block([[c, s], [-s, c]]))
    return np.concatenate([high, high, low], axis=0)


@functools.lru_cache(None)
def twiddle_table(length, orient):
    turns = np.outer(np.arange(digits), np.arange(lanes)) % length
    angle = orient * 2.0 * np.pi * turns / length
    return np.stack([np.cos(angle), np.sin(angle)]).astype(np.float32)


@functools.lru_cache(None)
def left_table(length, orient):
    index = np.arange(lanes)
    digit = np.arange(digits)
    turns = (digits * index[None, :, None] * index[None, None, :]
             + digit[:, None, None] * index[None, None, :]) % length
    if orient > 0:
        turns = np.swapaxes(turns, 1, 2)
    angle = orient * 2.0 * np.pi * turns / length
    c, s = np.cos(angle), np.sin(angle)
    full = np.concatenate([np.concatenate([c, -s], 2), np.concatenate([s, c], 2)], 1)
    high, low = split_pair(full)
    return np.concatenate([high, low], axis=2)


def four(a, b, c, d, orient):
    (ar, ai), (br, bi), (cr, ci), (dr, di) = a, b, c, d
    pr, pi = ar + cr, ai + ci
    mr, mi = ar - cr, ai - ci
    qr, qi = br + dr, bi + di
    nr, ni = br - dr, bi - di
    ir, ii = (-ni, nr) if orient > 0 else (ni, -nr)
    return [(pr + qr, pi + qi), (mr + ir, mi + ii), (pr - qr, pi - qi), (mr - ir, mi - ii)]


def turn16(value, step, orient):
    real, imag = value
    step = step % 16
    if step == 0:
        return value
    if step == 4:
        return (-imag, real) if orient > 0 else (imag, -real)
    root = float(np.sqrt(0.5))
    if step == 2:
        if orient > 0:
            return ((real - imag) * root, (real + imag) * root)
        return ((real + imag) * root, (imag - real) * root)
    if step == 6:
        if orient > 0:
            return ((real + imag) * -root, (real - imag) * root)
        return ((imag - real) * root, (real + imag) * -root)
    c = float(np.cos(2.0 * np.pi * step / 16))
    s = float(orient * np.sin(2.0 * np.pi * step / 16))
    return (real * c - imag * s, real * s + imag * c)


def sixteen(values, orient):
    inner = []
    for n2 in range(4):
        part = four(values[n2], values[4 + n2], values[8 + n2], values[12 + n2], orient)
        inner.append([turn16(part[k1], n2 * k1, orient) for k1 in range(4)])
    out = [None] * 16
    for k1 in range(4):
        part = four(inner[0][k1], inner[1][k1], inner[2][k1], inner[3][k1], orient)
        for k2 in range(4):
            out[k1 + 4 * k2] = part[k2]
    return out


def halves(value):
    high = value.astype(jnp.bfloat16)
    low = (value - high.astype(jnp.float32)).astype(jnp.bfloat16)
    return high, low


def times_right(value, table_ref):
    high, low = halves(value)
    wide = jnp.concatenate([high, low, high], axis=1)
    return jnp.dot(wide, table_ref[...], preferred_element_type=jnp.float32)


def times_left(table, value):
    high, low = halves(value)
    tall = jnp.concatenate([high, low, high], axis=0)
    wide = jnp.concatenate([table[:, :2 * lanes], table[:, :2 * lanes], table[:, 2 * lanes:]], axis=1)
    return jnp.dot(wide, tall, preferred_element_type=jnp.float32)


sine_terms = [(-1.0) ** n / math.factorial(2 * n + 1) for n in range(6)]
cosine_terms = [(-1.0) ** n / math.factorial(2 * n) for n in range(7)]
pi_high = float(np.float32(np.pi).astype(jnp.bfloat16))
pi_low = float(np.pi - pi_high)


def series(terms, square):
    total = square * terms[-1] + terms[-2]
    for term in reversed(terms[:-2]):
        total = total * square + term
    return total


def cos_sin(angle):
    turns = jnp.floor(angle * (1.0 / np.pi) + 0.5)
    rest = (angle - turns * pi_high) - turns * pi_low
    flip = 1.0 - 2.0 * (turns - 2.0 * jnp.floor(turns * 0.5))
    square = rest * rest
    return flip * series(cosine_terms, square), flip * rest * series(sine_terms, square)


def product(a, b):
    return (a[0] * b[0] - a[1] * b[1], a[0] * b[1] + a[1] * b[0])


shards = 8


def block_shapes(rows):
    return [jax.ShapeDtypeStruct((2, 2, rows, lanes), jnp.float32)] * shards


def block_specs(rows):
    return [pl.BlockSpec((2, 2, rows, lanes), lambda i, *_: (0, 0, i, 0))] * shards


def swap(array, axis, mask):
    size = lax.axis_size(axis)
    return lax.ppermute(array, axis, [(d, d ^ mask) for d in range(size)])


def after(value, *others):
    return lax.optimization_barrier((value, *others))[0]


def exchange(blocks, gate=None):
    if gate is not None:
        blocks = [blocks[0]] + [after(block, seen) for block, seen in zip(blocks[1:], gate[1:])]
    return [blocks[0]] + [swap(block, "row", k) for k, block in enumerate(blocks) if k]


def to_last_wavenumbers(me, held, table_ref, outs):
    rows = held.shape[1]
    for k in range(shards):
        done = times_right(held[pl.ds((me ^ k) * 2, 2)].reshape(2 * rows, 2 * lanes), table_ref)
        for j in range(2):
            for c in range(2):
                outs[k][j, c] = done[j * rows:(j + 1) * rows, c * lanes:(c + 1) * lanes]


def forward_last_kernel(me_ref, x_ref, twid_ref, table_ref, *rest):
    outs, held = rest[:-1], rest[-1]
    rows = x_ref.shape[1]

    def one(t, carry):
        at = pl.ds(pl.multiple_of(t * sub, sub), sub)
        values = [
            (x_ref[0, at, a * lanes:(a + 1) * lanes], x_ref[1, at, a * lanes:(a + 1) * lanes])
            for a in range(digits)
        ]
        for q, value in enumerate(sixteen(values, -1)):
            if q:
                value = product(value, (twid_ref[0, q:q + 1, :], twid_ref[1, q:q + 1, :]))
            held[q, at, :lanes] = value[0]
            held[q, at, lanes:] = value[1]
        return carry

    lax.fori_loop(0, rows // sub, one, 0)
    to_last_wavenumbers(me_ref[0], held, table_ref, outs)


def light():
    return pl.CostEstimate(flops=1000, bytes_accessed=1000, transcendentals=0)


def smem():
    return pl.BlockSpec(memory_space=pltpu.SMEM)


def whole(table):
    return pl.BlockSpec(table.shape, lambda i, *_: (0,) * table.ndim)


def params():
    return pltpu.CompilerParams(vmem_limit_bytes=vmem_bytes)


def forward_last(me, field, chunk):
    _, rows, cols = field.shape
    twid = twiddle_table(cols, -1)
    table = right_table(-1)
    return pl.pallas_call(
        forward_last_kernel,
        grid=(rows // chunk,),
        in_specs=[
            smem(),
            pl.BlockSpec((2, chunk, cols), lambda i: (0, i, 0)),
            whole(twid),
            whole(table),
        ],
        out_specs=block_specs(chunk),
        out_shape=block_shapes(rows),
        scratch_shapes=[pltpu.VMEM((digits, chunk, 2 * lanes), jnp.float32)],
        compiler_params=params(),
        cost_estimate=light(),
        name="forward_last",
    )(me, field, twid, table)


def middle_kernel(sign, pieces, me_ref, fwd_ref, inv_ref, mr_ref, mi_ref, *rest):
    ins, (held, spare) = rest[:shards], rest[-2:]
    outs = rest[-2 - shards * max(len(pieces), 1):-2]
    me = me_ref[0]
    step, steps = pl.program_id(0), digits // fwd_ref.shape[0]

    @pl.when(step == 0)
    def _():
        along_first(me, ins, held, spare)

    def second(n, carry):
        q = step * fwd_ref.shape[0] + n
        spec = times_left(fwd_ref[n], held[q])
        real, imag = spec[:lanes], spec[lanes:]
        mr, mi = mr_ref[n], mi_ref[n]
        if sign > 0:
            moved = (real * mr - imag * mi, real * mi + imag * mr)
        else:
            moved = (real * mr + imag * mi, imag * mr - real * mi)
        held[q] = times_left(inv_ref[n], jnp.concatenate(moved, axis=0))
        return carry

    lax.fori_loop(0, fwd_ref.shape[0], second, 0)

    @pl.when(step == steps - 1)
    def _():
        along_last(me, pieces, outs, held, spare)


def along_first(me, ins, held, spare):
    for j in range(2):
        col = slice(j * lanes, (j + 1) * lanes)
        for k in range(shards):
            for n in range(2):
                spare[(me ^ k) * 2 + n, :, :, col] = ins[k][j, :, n * lanes:(n + 1) * lanes, :]

    def first(t, carry):
        base = pl.multiple_of(t // 2 * sub, sub)
        col = pl.ds(pl.multiple_of(t % 2 * lanes, lanes), lanes)
        at = pl.ds(base, sub)
        values = [(spare[a, 0, at, col], spare[a, 1, at, col]) for a in range(digits)]
        for q, value in enumerate(sixteen(values, -1)):
            held[q, at, col] = value[0]
            held[q, pl.ds(lanes + base, sub), col] = value[1]
        return carry

    lax.fori_loop(0, 2 * lanes // sub, first, 0)


def along_last(me, pieces, outs, held, spare):
    def third(t, carry):
        base = pl.multiple_of(t // 2 * sub, sub)
        col = pl.ds(pl.multiple_of(t % 2 * lanes, lanes), lanes)
        at = pl.ds(base, sub)
        values = [(held[q, at, col], held[q, pl.ds(lanes + base, sub), col]) for q in range(digits)]
        for a, value in enumerate(sixteen(values, 1)):
            spare[a, 0, at, col] = value[0]
            spare[a, 1, at, col] = value[1]
        return carry

    lax.fori_loop(0, 2 * lanes // sub, third, 0)
    start = 0
    for p, size in enumerate(pieces or (outs[0].shape[2],)):
        at = 0
        while at < size:
            n, r = (start + at) // lanes, (start + at) % lanes
            span = min(size - at, lanes - r)
            for k in range(shards):
                for j in range(2):
                    col = slice(j * lanes, (j + 1) * lanes)
                    value = spare[(me ^ k) * 2 + n, :, r:r + span, col]
                    if pieces:
                        outs[p * shards + k][0, j, :, at:at + span] = value
                    else:
                        outs[k][j, :, at:at + span] = value
            at += span
        start += size


def middle(me, blocks, mult, sign, pieces=(), into=None):
    rows = blocks[0].shape[2]
    length = shards * rows
    fwd, inv = left_table(length, -1), left_table(length, 1)
    operands = [me, fwd, inv, *mult, *blocks]
    steps = 4

    def by_step(table):
        return pl.BlockSpec((digits // steps,) + table.shape[1:], lambda i: (i, 0, 0))

    in_specs = [smem(), by_step(fwd), by_step(inv), by_step(mult[0]), by_step(mult[1])]
    in_specs += [pl.BlockSpec((2, 2, rows, lanes), lambda i: (0, 0, 0, 0))] * shards
    aliases = {}
    out_specs = [pl.BlockSpec((2, 2, rows, lanes), lambda i: (0, 0, 0, 0))] * shards
    out_shape = block_shapes(rows)
    if pieces:
        out_specs, out_shape = [], []
        for p, (size, fields, place) in enumerate(pieces):
            for k in range(shards):
                out_specs.append(pl.BlockSpec((1, 2, 2, size, lanes), lambda i, place=place: (place, 0, 0, 0, 0)))
                out_shape.append(jax.ShapeDtypeStruct((fields, 2, 2, size, lanes), jnp.float32))
                if place:
                    aliases[len(operands)] = p * shards + k
                    operands.append(into[p][k])
                    in_specs.append(pl.BlockSpec(memory_space=pl.ANY))
    outs = pl.pallas_call(
        functools.partial(middle_kernel, sign, tuple(size for size, _, _ in pieces)),
        grid=(steps,),
        in_specs=in_specs,
        out_specs=out_specs,
        out_shape=out_shape,
        input_output_aliases=aliases,
        scratch_shapes=[
            pltpu.VMEM((digits, 2 * lanes, 2 * lanes), jnp.float32),
            pltpu.VMEM((digits, 2, lanes, 2 * lanes), jnp.float32),
        ],
        compiler_params=params(),
        cost_estimate=light(),
        name="middle",
    )(*operands)
    return [outs[p * shards:(p + 1) * shards] for p in range(len(pieces))] if pieces else outs


def space_kernel(sign, onward, keep, image, aliased, *refs):
    refs = list(refs[1:])
    me = refs.pop(0)[0]
    if image == "halves":
        bit = refs.pop(0)[0]
    scale_ref, slow_ref, itwid_ref, itable_ref = refs[:4]
    del refs[:4]
    scale = scale_ref[0]
    ins = refs[:shards]
    del refs[:shards]
    if image:
        other_ref = refs.pop(0)
    if onward:
        twid_ref, table_ref = refs[:2]
        del refs[:2]
    if aliased:
        refs.pop(0)
    field_ref = refs.pop(0) if keep else None
    if onward:
        outs = refs[:shards]
        del refs[:shards]
    if image == "halves":
        mine_ref, theirs_ref, held, image_ref = refs
    elif image:
        image_ref, held = refs
    else:
        (held,) = refs
    rows = held.shape[1]

    for k in range(shards):
        block = ins[k][0] if len(ins[k].shape) == 5 else ins[k][...]
        wide = [jnp.concatenate([block[j, 0], block[j, 1]], axis=1) for j in range(2)]
        done = times_right(jnp.concatenate(wide, axis=0), itable_ref)
        held[pl.ds((me ^ k) * 2, 2)] = done.reshape(2, rows, 2 * lanes)

    def one(t, carry):
        at = pl.ds(pl.multiple_of(t * sub, sub), sub)
        values = []
        for q in range(digits):
            value = (held[q, at, :lanes], held[q, at, lanes:])
            if q:
                value = product(value, (itwid_ref[0, q:q + 1, :], itwid_ref[1, q:q + 1, :]))
            values.append(value)
        values = sixteen(values, 1)
        for a in range(digits):
            real, imag = values[a]
            col = slice(a * lanes, (a + 1) * lanes)
            c, s = cos_sin(scale * slow_ref[0, at, col])
            if sign > 0:
                real, imag = real * c - imag * s, real * s + imag * c
            else:
                real, imag = real * c + imag * s, imag * c - real * s
            if keep:
                field_ref[0, at, col] = real
                field_ref[1, at, col] = imag
            if image:
                image_ref[at, col] = real * other_ref[0, at, col] + imag * other_ref[1, at, col]
            values[a] = (real, imag)
        if onward:
            for q, value in enumerate(sixteen(values, -1)):
                if q:
                    value = product(value, (twid_ref[0, q:q + 1, :], twid_ref[1, q:q + 1, :]))
                held[q, at, :lanes] = value[0]
                held[q, at, lanes:] = value[1]
        return carry

    lax.fori_loop(0, rows // sub, one, 0)
    if image == "halves":
        half = rows // 2
        mine_ref[...] = image_ref[pl.ds(pl.multiple_of(bit * half, sub), half), :]
        theirs_ref[...] = image_ref[pl.ds(pl.multiple_of((1 - bit) * half, sub), half), :]
    if onward:
        to_last_wavenumbers(me, held, table_ref, outs)


def space(me, blocks, scale, slow, store_pos, z, sign, onward, other=None, keep=True, start=0, into=None, bit=None, chunk=128, part=None, skip=0):
    _, rows, cols = slow.shape
    if isinstance(blocks, tuple):
        blocks, place = blocks
        part = part or blocks[0].shape[3]
        chunk = min(chunk, part)
        over = skip // chunk
        specs = [pl.BlockSpec((1, 2, 2, chunk, lanes), lambda i, *_: (place, 0, 0, over + i, 0))] * shards
    else:
        part = blocks[0].shape[2]
        specs = block_specs(chunk)
    first = start // chunk
    image = None if other is None else "whole" if bit is None else "halves"
    itwid, itable = twiddle_table(cols, 1), right_table(1)
    field_spec = pl.BlockSpec((2, chunk, cols), lambda i, *_: (0, first + i, 0))
    slow_spec = pl.BlockSpec((1, chunk, cols), lambda i, at: (at[z], first + i, 0))
    operands, in_specs = [store_pos, me], [smem()]
    if image == "halves":
        operands.append(bit)
        in_specs.append(smem())
    operands += [scale, slow, itwid, itable]
    in_specs += [smem(), slow_spec, whole(itwid), whole(itable)]
    operands += blocks
    in_specs += specs
    if image:
        operands.append(other)
        in_specs.append(field_spec)
    if onward:
        tables = [twiddle_table(cols, -1), right_table(-1)]
        operands += tables
        in_specs += [whole(table) for table in tables]
    aliases = {}
    if into is not None:
        aliases = {len(operands): 0}
        operands.append(into)
        in_specs.append(pl.BlockSpec(memory_space=pl.ANY))
    out_specs, out_shape = [], []
    scratch = [pltpu.VMEM((digits, chunk, 2 * lanes), jnp.float32)]
    if keep:
        out_specs.append(field_spec)
        out_shape.append(jax.ShapeDtypeStruct((2, rows, cols), jnp.float32))
    if onward:
        out_specs += block_specs(chunk)
        out_shape += block_shapes(part)
    if image == "whole":
        out_specs.append(pl.BlockSpec((chunk, cols), lambda i, *_: (i, 0)))
        out_shape.append(jax.ShapeDtypeStruct((part, cols), jnp.float32))
    elif image:
        out_specs += [pl.BlockSpec((chunk // 2, cols), lambda i, *_: (i, 0))] * 2
        out_shape += [jax.ShapeDtypeStruct((part // 2, cols), jnp.float32)] * 2
        scratch.append(pltpu.VMEM((chunk, cols), jnp.float32))
    outs = pl.pallas_call(
        functools.partial(space_kernel, sign, onward, keep, image, into is not None),
        grid_spec=pltpu.PrefetchScalarGridSpec(
            num_scalar_prefetch=1,
            grid=(part // chunk,),
            in_specs=in_specs,
            out_specs=out_specs,
            scratch_shapes=scratch,
        ),
        out_shape=out_shape,
        input_output_aliases=aliases,
        compiler_params=params(),
        cost_estimate=light(),
        name="space",
    )(*operands)
    outs = list(outs)
    field = outs.pop(0) if keep else None
    onward_blocks = outs[:shards] if onward else None
    if image == "halves":
        term = outs[-2:]
    else:
        term = outs[-1] if image else None
    return field, onward_blocks, term


def put_kernel(halved, bit_ref, *refs):
    refs, out_ref = list(refs), refs[-1]
    bit = bit_ref[0]
    at = 0
    for two in halved:
        size = refs[0].shape[0]
        if two:
            mine, theirs = refs.pop(0), refs.pop(0)
            out_ref[0, pl.ds(pl.multiple_of(at + bit * size, sub), size), :] = mine[...]
            out_ref[0, pl.ds(pl.multiple_of(at + (1 - bit) * size, sub), size), :] = theirs[...]
            at += 2 * size
        else:
            out_ref[0, at:at + size, :] = refs.pop(0)[...]
            at += size


def put(image, z, bit, sums):
    flat = []
    for value in sums:
        flat += list(value) if isinstance(value, tuple) else [value]
    in_specs = [smem()] + [whole(v) for v in flat]
    operands = [bit, *flat]
    aliases = {}
    if isinstance(image, tuple):
        shape = image
    else:
        shape = image.shape
        aliases = {len(operands): 0}
        operands.append(image)
        in_specs.append(pl.BlockSpec(memory_space=pl.ANY))
    return pl.pallas_call(
        functools.partial(put_kernel, [isinstance(value, tuple) for value in sums]),
        grid=(1,),
        in_specs=in_specs,
        out_specs=pl.BlockSpec((1,) + shape[1:], lambda i: (z, 0, 0)),
        out_shape=jax.ShapeDtypeStruct(shape, jnp.float32),
        input_output_aliases=aliases,
        compiler_params=params(),
        cost_estimate=light(),
        name="put",
    )(*operands)


def wavenumber(index, length):
    signed = jnp.where(index < length // 2, index, index - length)
    return 2.0 * jnp.pi * (signed.astype(jnp.float32) / length)


def multiplier(omega, kx_index, ky_index, rows_total, cols_total):
    kx_values = wavenumber(kx_index, rows_total)
    ky_values = wavenumber(ky_index, cols_total)
    phase_q = omega * omega - (kx_values * kx_values + ky_values * ky_values)
    travel = jnp.sqrt(jnp.maximum(phase_q, 0.0))
    decay = jnp.sqrt(jnp.maximum(-phase_q, 0.0))
    damping = jnp.exp(-depth_step * decay) / (rows_total * cols_total)
    return damping * jnp.cos(depth_step * travel), damping * jnp.sin(depth_step * travel)


def on_device(source_field, receiver_field, slowness_store, store_pos, freq_index):
    omega = omega_unit * freq_index.astype(jnp.float32)[0]
    rows = source_field.shape[2]
    cols = source_field.shape[3]
    rows_total = rows * 8
    me = lax.axis_index("row").astype(jnp.int32)[None]
    bit = lax.axis_index("freq").astype(jnp.int32)[None] & 1

    grid_shape = (digits, lanes, 2 * lanes)
    kx_index = lax.broadcasted_iota(jnp.int32, grid_shape, 0) + digits * lax.broadcasted_iota(
        jnp.int32, grid_shape, 1
    )
    column = lax.broadcasted_iota(jnp.int32, grid_shape, 2)
    ky_index = lax.axis_index("row") * 2 + column // lanes + digits * (column % lanes)
    def behind(*arrays):
        return after(me, *arrays)

    spec_source = forward_last(me, source_field[0], 128)
    moved_source = exchange(spec_source)
    slow = lax.all_gather(slowness_store, "freq", axis=0, tiled=True)
    mult = multiplier(after(omega, *moved_source), kx_index, ky_index, rows_total, cols)

    scale = (depth_step * omega)[None]

    spec_receiver = forward_last(behind(moved_source[1]), receiver_field[0], 128)
    moved_receiver = exchange(spec_receiver, moved_source)
    mid_source = middle(behind(spec_receiver[0]), moved_source, mult, -1)
    mid_receiver = middle(behind(mid_source[0]), moved_receiver, mult, 1)
    back_source = exchange(mid_source, moved_receiver)
    back_receiver = exchange(mid_receiver, back_source)
    source_now, spec_source, _ = space(behind(mid_receiver[0]), back_source, scale, slow, store_pos, 0, -1, True)
    _, spec_receiver, term = space(me, back_receiver, scale, slow, store_pos, 0, 1, True, other=source_now, keep=False)
    first_image = lax.psum(term, "freq")

    moved_source = exchange(spec_source, back_receiver)
    moved_receiver = exchange(spec_receiver, moved_source)
    sizes = (rows // 2, rows // 2)
    mid_source = middle(
        behind(spec_receiver[0]), moved_source, mult, -1,
        tuple((size, min(n, 1) + 1, 0) for n, size in enumerate(sizes)),
    )
    image = put((DEPTHS, rows, cols), 0, bit, [first_image])
    mid_receiver = middle(
        me, moved_receiver, mult, 1, tuple((size, min(n, 1) + 1, min(n, 1)) for n, size in enumerate(sizes)),
        mid_source,
    )
    late = [after(block, mid_receiver[0][0]) for block in mid_source[0][1:3]]
    first_source = exchange([mid_source[0][0], *late, *mid_source[0][3:]], moved_receiver)
    moved = exchange(mid_receiver[0], first_source)

    def finish(tie, back_source, back_receiver, start, source_now, receiver_now, part, skip):
        source_now, _, _ = space(
            tie, back_source, scale, slow, store_pos, 1, -1, False, start=start, into=source_now, part=part, skip=skip
        )
        receiver_now, _, term = space(
            me, back_receiver, scale, slow, store_pos, 1, 1, False, other=source_now, start=start,
            into=receiver_now, bit=bit, part=part, skip=skip,
        )
        return source_now, receiver_now, term

    def near_sum(term, *marks):
        mine, theirs = term
        return mine + swap(after(theirs, *marks) if marks else theirs, "freq", 1)

    def far_sum(value, *marks):
        value = after(value, *marks) if marks else value
        return value + swap(value, "freq", 2)

    half, quarter = rows // 2, rows // 4
    source_now, receiver_now, term = finish(
        behind(image), (first_source, 0), (moved, 0), 0, None, None, half, 0
    )
    blocks = mid_receiver[1]
    blocks = [blocks[0], *[after(block, term[0]) for block in blocks[1:3]], *blocks[3:]]
    moved = exchange(blocks, moved)
    pair = ((moved, 0), (moved, 1))
    near = [near_sum(term)]
    far = [far_sum(near[0])]
    source_now, receiver_now, term = finish(
        behind(near[0]), *pair, half, source_now, receiver_now, quarter, 0
    )
    back = [swap(far[0], "freq", 1)]
    near.append(near_sum(term))
    source_now, receiver_now, term = finish(
        behind(near[0]), *pair, half + quarter, source_now, receiver_now, quarter, quarter
    )
    far.append(far_sum(near[1]))
    near.append(near_sum(term, far[0], near[1]))
    far.append(far_sum(near[2], back[0]))
    back += [swap(value, "freq", 1) for value in far[1:]]
    return put(image, 1, bit, list(zip(far, back))), source_now[None], receiver_now[None]


def plain_step(field, mult_real, mult_imag):
    def table(length, orient):
        index = lax.broadcasted_iota(jnp.int32, (length, length), 0) * lax.broadcasted_iota(
            jnp.int32, (length, length), 1
        )
        angle = 2.0 * jnp.pi / length * (index % length).astype(jnp.float32)
        return jnp.cos(angle), orient * jnp.sin(angle)

    def along(real, imag, orient, last):
        c, s = table(real.shape[1 if last else 0], orient)
        dot = functools.partial(jnp.matmul, precision=lax.Precision.HIGHEST)
        if last:
            return dot(real, c) - dot(imag, s), dot(real, s) + dot(imag, c)
        return dot(c, real) - dot(s, imag), dot(s, real) + dot(c, imag)

    def trade(pair, split, join):
        both = lax.all_to_all(jnp.stack(pair), "row", split_axis=split, concat_axis=join, tiled=True)
        return both[0], both[1]

    real, imag = along(field[0], field[1], -1.0, True)
    real, imag = trade((real, imag), 2, 1)
    real, imag = along(real, imag, -1.0, False)
    real, imag = product((real, imag), (mult_real, mult_imag))
    real, imag = along(real, imag, 1.0, False)
    real, imag = trade((real, imag), 1, 2)
    return jnp.stack(along(real, imag, 1.0, True))


def on_device_plain(source_field, receiver_field, slowness_store, store_pos, freq_index):
    omega = omega_unit * freq_index.astype(jnp.float32)[0]
    rows = source_field.shape[2]
    cols = source_field.shape[3]
    shards = lax.axis_size("row")
    rows_total = rows * shards
    block = cols // shards
    slow = lax.all_gather(slowness_store, "freq", axis=0, tiled=True)
    kx_index = lax.broadcasted_iota(jnp.int32, (rows_total, block), 0)
    ky_index = lax.broadcasted_iota(jnp.int32, (rows_total, block), 1) + lax.axis_index("row") * block
    mult_real, mult_imag = multiplier(omega, kx_index, ky_index, rows_total, cols)
    source_now, receiver_now = source_field[0], receiver_field[0]
    images = []
    for z in range(DEPTHS):
        angles = depth_step * omega * slow[store_pos[z]]
        lens_cos, lens_sin = jnp.cos(angles), jnp.sin(angles)
        source_now = plain_step(source_now, mult_real, -mult_imag)
        receiver_now = plain_step(receiver_now, mult_real, mult_imag)
        source_now = jnp.stack(product(source_now, (lens_cos, -lens_sin)))
        receiver_now = jnp.stack(product(receiver_now, (lens_cos, lens_sin)))
        images.append(lax.psum(jnp.sum(source_now * receiver_now, axis=0), "freq"))
    return jnp.stack(images), source_now[None], receiver_now[None]


def solution(mesh):
    placed = (
        P("freq", None, "row", None),
        P("freq", None, "row", None),
        P("freq", "row", None),
        P(),
        P("freq"),
    )

    def chosen(source_field, *rest):
        rows, cols = source_field.shape[2:]
        split = lax.axis_size("row")
        length = digits * lanes
        fits = split == shards and lax.axis_size("freq") == 4 and cols == length and rows * split == length
        return (on_device if fits else on_device_plain)(source_field, *rest)

    return jax.shard_map(
        chosen,
        mesh=mesh,
        in_specs=placed,
        out_specs=(
            P(None, "row", None),
            P("freq", None, "row", None),
            P("freq", None, "row", None),
        ),
        check_vma=False,
    )
```

```python
import functools
import math

import jax
import jax.numpy as jnp
import numpy as np
from jax import lax
from jax.experimental import pallas as pl
from jax.experimental.pallas import tpu as pltpu
from jax.sharding import PartitionSpec as P

DEPTHS = 2


depth_step = 16.0
omega_unit = 0.045
lanes = 128
digits = 16
sub = 8
vmem_bytes = 60 * 1024 * 1024


def split_pair(table):
    high = table.astype(jnp.bfloat16)
    low = (table - high.astype(np.float64)).astype(jnp.bfloat16)
    return high, low


@functools.lru_cache(None)
def right_table(orient):
    index = np.arange(lanes)
    angle = orient * 2.0 * np.pi * (np.outer(index, index) % lanes) / lanes
    c, s = np.cos(angle), np.sin(angle)
    high, low = split_pair(np.block([[c, s], [-s, c]]))
    return np.concatenate([high, high, low], axis=0)


@functools.lru_cache(None)
def twiddle_table(length, orient):
    turns = np.outer(np.arange(digits), np.arange(lanes)) % length
    angle = orient * 2.0 * np.pi * turns / length
    return np.stack([np.cos(angle), np.sin(angle)]).astype(np.float32)


@functools.lru_cache(None)
def left_table(length, orient):
    index = np.arange(lanes)
    digit = np.arange(digits)
    turns = (digits * index[None, :, None] * index[None, None, :]
             + digit[:, None, None] * index[None, None, :]) % length
    if orient > 0:
        turns = np.swapaxes(turns, 1, 2)
    angle = orient * 2.0 * np.pi * turns / length
    c, s = np.cos(angle), np.sin(angle)
    full = np.concatenate([np.concatenate([c, -s], 2), np.concatenate([s, c], 2)], 1)
    high, low = split_pair(full)
    return np.concatenate([high, low], axis=2)


def four(a, b, c, d, orient):
    (ar, ai), (br, bi), (cr, ci), (dr, di) = a, b, c, d
    pr, pi = ar + cr, ai + ci
    mr, mi = ar - cr, ai - ci
    qr, qi = br + dr, bi + di
    nr, ni = br - dr, bi - di
    ir, ii = (-ni, nr) if orient > 0 else (ni, -nr)
    return [(pr + qr, pi + qi), (mr + ir, mi + ii), (pr - qr, pi - qi), (mr - ir, mi - ii)]


def turn16(value, step, orient):
    real, imag = value
    step = step % 16
    if step == 0:
        return value
    if step == 4:
        return (-imag, real) if orient > 0 else (imag, -real)
    root = float(np.sqrt(0.5))
    if step == 2:
        if orient > 0:
            return ((real - imag) * root, (real + imag) * root)
        return ((real + imag) * root, (imag - real) * root)
    if step == 6:
        if orient > 0:
            return ((real + imag) * -root, (real - imag) * root)
        return ((imag - real) * root, (real + imag) * -root)
    c = float(np.cos(2.0 * np.pi * step / 16))
    s = float(orient * np.sin(2.0 * np.pi * step / 16))
    return (real * c - imag * s, real * s + imag * c)


def sixteen(values, orient):
    inner = []
    for n2 in range(4):
        part = four(values[n2], values[4 + n2], values[8 + n2], values[12 + n2], orient)
        inner.append([turn16(part[k1], n2 * k1, orient) for k1 in range(4)])
    out = [None] * 16
    for k1 in range(4):
        part = four(inner[0][k1], inner[1][k1], inner[2][k1], inner[3][k1], orient)
        for k2 in range(4):
            out[k1 + 4 * k2] = part[k2]
    return out


def halves(value):
    high = value.astype(jnp.bfloat16)
    low = (value - high.astype(jnp.float32)).astype(jnp.bfloat16)
    return high, low


def times_right(value, table_ref):
    high, low = halves(value)
    wide = jnp.concatenate([high, low, high], axis=1)
    return jnp.dot(wide, table_ref[...], preferred_element_type=jnp.float32)


def times_left(table, value):
    high, low = halves(value)
    tall = jnp.concatenate([high, low, high], axis=0)
    wide = jnp.concatenate([table[:, :2 * lanes], table[:, :2 * lanes], table[:, 2 * lanes:]], axis=1)
    return jnp.dot(wide, tall, preferred_element_type=jnp.float32)


sine_terms = [(-1.0) ** n / math.factorial(2 * n + 1) for n in range(6)]
cosine_terms = [(-1.0) ** n / math.factorial(2 * n) for n in range(7)]
pi_high = float(np.float32(np.pi).astype(jnp.bfloat16))
pi_low = float(np.pi - pi_high)


def series(terms, square):
    total = square * terms[-1] + terms[-2]
    for term in reversed(terms[:-2]):
        total = total * square + term
    return total


def cos_sin(angle):
    turns = jnp.floor(angle * (1.0 / np.pi) + 0.5)
    rest = (angle - turns * pi_high) - turns * pi_low
    flip = 1.0 - 2.0 * (turns - 2.0 * jnp.floor(turns * 0.5))
    square = rest * rest
    return flip * series(cosine_terms, square), flip * rest * series(sine_terms, square)


def product(a, b):
    return (a[0] * b[0] - a[1] * b[1], a[0] * b[1] + a[1] * b[0])


shards = 8


def block_shapes(rows):
    return [jax.ShapeDtypeStruct((2, 2, rows, lanes), jnp.float32)] * shards


def block_specs(rows):
    return [pl.BlockSpec((2, 2, rows, lanes), lambda i, *_: (0, 0, i, 0))] * shards


def swap(array, axis, mask):
    size = lax.axis_size(axis)
    return lax.ppermute(array, axis, [(d, d ^ mask) for d in range(size)])


def after(value, *others):
    return lax.optimization_barrier((value, *others))[0]


def exchange(blocks, gate=None):
    if gate is not None:
        blocks = [blocks[0]] + [after(block, seen) for block, seen in zip(blocks[1:], gate[1:])]
    return [blocks[0]] + [swap(block, "row", k) for k, block in enumerate(blocks) if k]


def to_last_wavenumbers(me, held, table_ref, outs):
    rows = held.shape[1]
    for k in range(shards):
        done = times_right(held[pl.ds((me ^ k) * 2, 2)].reshape(2 * rows, 2 * lanes), table_ref)
        for j in range(2):
            for c in range(2):
                outs[k][j, c] = done[j * rows:(j + 1) * rows, c * lanes:(c + 1) * lanes]


def forward_last_kernel(me_ref, x_ref, twid_ref, table_ref, *rest):
    outs, held = rest[:-1], rest[-1]
    rows = x_ref.shape[1]

    def one(t, carry):
        at = pl.ds(pl.multiple_of(t * sub, sub), sub)
        values = [
            (x_ref[0, at, a * lanes:(a + 1) * lanes], x_ref[1, at, a * lanes:(a + 1) * lanes])
            for a in range(digits)
        ]
        for q, value in enumerate(sixteen(values, -1)):
            if q:
                value = product(value, (twid_ref[0, q:q + 1, :], twid_ref[1, q:q + 1, :]))
            held[q, at, :lanes] = value[0]
            held[q, at, lanes:] = value[1]
        return carry

    lax.fori_loop(0, rows // sub, one, 0)
    to_last_wavenumbers(me_ref[0], held, table_ref, outs)


def light():
    return pl.CostEstimate(flops=1000, bytes_accessed=1000, transcendentals=0)


def smem():
    return pl.BlockSpec(memory_space=pltpu.SMEM)


def whole(table):
    return pl.BlockSpec(table.shape, lambda i, *_: (0,) * table.ndim)


def params():
    return pltpu.CompilerParams(vmem_limit_bytes=vmem_bytes)


def forward_last(me, field, chunk):
    _, rows, cols = field.shape
    twid = twiddle_table(cols, -1)
    table = right_table(-1)
    return pl.pallas_call(
        forward_last_kernel,
        grid=(rows // chunk,),
        in_specs=[
            smem(),
            pl.BlockSpec((2, chunk, cols), lambda i: (0, i, 0)),
            whole(twid),
            whole(table),
        ],
        out_specs=block_specs(chunk),
        out_shape=block_shapes(rows),
        scratch_shapes=[pltpu.VMEM((digits, chunk, 2 * lanes), jnp.float32)],
        compiler_params=params(),
        cost_estimate=light(),
        name="forward_last",
    )(me, field, twid, table)


def middle_kernel(sign, pieces, me_ref, fwd_ref, inv_ref, mr_ref, mi_ref, *rest):
    ins, (held, spare) = rest[:shards], rest[-2:]
    outs = rest[-2 - shards * max(len(pieces), 1):-2]
    me = me_ref[0]
    step, steps = pl.program_id(0), digits // fwd_ref.shape[0]

    @pl.when(step == 0)
    def _():
        along_first(me, ins, held, spare)

    def second(n, carry):
        q = step * fwd_ref.shape[0] + n
        spec = times_left(fwd_ref[n], held[q])
        real, imag = spec[:lanes], spec[lanes:]
        mr, mi = mr_ref[n], mi_ref[n]
        if sign > 0:
            moved = (real * mr - imag * mi, real * mi + imag * mr)
        else:
            moved = (real * mr + imag * mi, imag * mr - real * mi)
        held[q] = times_left(inv_ref[n], jnp.concatenate(moved, axis=0))
        return carry

    lax.fori_loop(0, fwd_ref.shape[0], second, 0)

    @pl.when(step == steps - 1)
    def _():
        along_last(me, pieces, outs, held, spare)


def along_first(me, ins, held, spare):
    for j in range(2):
        col = slice(j * lanes, (j + 1) * lanes)
        for k in range(shards):
            for n in range(2):
                spare[(me ^ k) * 2 + n, :, :, col] = ins[k][j, :, n * lanes:(n + 1) * lanes, :]

    def first(t, carry):
        base = pl.multiple_of(t // 2 * sub, sub)
        col = pl.ds(pl.multiple_of(t % 2 * lanes, lanes), lanes)
        at = pl.ds(base, sub)
        values = [(spare[a, 0, at, col], spare[a, 1, at, col]) for a in range(digits)]
        for q, value in enumerate(sixteen(values, -1)):
            held[q, at, col] = value[0]
            held[q, pl.ds(lanes + base, sub), col] = value[1]
        return carry

    lax.fori_loop(0, 2 * lanes // sub, first, 0)


def along_last(me, pieces, outs, held, spare):
    def third(t, carry):
        base = pl.multiple_of(t // 2 * sub, sub)
        col = pl.ds(pl.multiple_of(t % 2 * lanes, lanes), lanes)
        at = pl.ds(base, sub)
        values = [(held[q, at, col], held[q, pl.ds(lanes + base, sub), col]) for q in range(digits)]
        for a, value in enumerate(sixteen(values, 1)):
            spare[a, 0, at, col] = value[0]
            spare[a, 1, at, col] = value[1]
        return carry

    lax.fori_loop(0, 2 * lanes // sub, third, 0)
    start = 0
    for p, size in enumerate(pieces or (outs[0].shape[2],)):
        at = 0
        while at < size:
            n, r = (start + at) // lanes, (start + at) % lanes
            span = min(size - at, lanes - r)
            for k in range(shards):
                for j in range(2):
                    col = slice(j * lanes, (j + 1) * lanes)
                    value = spare[(me ^ k) * 2 + n, :, r:r + span, col]
                    if pieces:
                        outs[p * shards + k][0, j, :, at:at + span] = value
                    else:
                        outs[k][j, :, at:at + span] = value
            at += span
        start += size


def middle(me, blocks, mult, sign, pieces=(), into=None):
    rows = blocks[0].shape[2]
    length = shards * rows
    fwd, inv = left_table(length, -1), left_table(length, 1)
    operands = [me, fwd, inv, *mult, *blocks]
    steps = 4

    def by_step(table):
        return pl.BlockSpec((digits // steps,) + table.shape[1:], lambda i: (i, 0, 0))

    in_specs = [smem(), by_step(fwd), by_step(inv), by_step(mult[0]), by_step(mult[1])]
    in_specs += [pl.BlockSpec((2, 2, rows, lanes), lambda i: (0, 0, 0, 0))] * shards
    aliases = {}
    out_specs = [pl.BlockSpec((2, 2, rows, lanes), lambda i: (0, 0, 0, 0))] * shards
    out_shape = block_shapes(rows)
    if pieces:
        out_specs, out_shape = [], []
        for p, (size, fields, place) in enumerate(pieces):
            for k in range(shards):
                out_specs.append(pl.BlockSpec((1, 2, 2, size, lanes), lambda i, place=place: (place, 0, 0, 0, 0)))
                out_shape.append(jax.ShapeDtypeStruct((fields, 2, 2, size, lanes), jnp.float32))
                if place:
                    aliases[len(operands)] = p * shards + k
                    operands.append(into[p][k])
                    in_specs.append(pl.BlockSpec(memory_space=pl.ANY))
    outs = pl.pallas_call(
        functools.partial(middle_kernel, sign, tuple(size for size, _, _ in pieces)),
        grid=(steps,),
        in_specs=in_specs,
        out_specs=out_specs,
        out_shape=out_shape,
        input_output_aliases=aliases,
        scratch_shapes=[
            pltpu.VMEM((digits, 2 * lanes, 2 * lanes), jnp.float32),
            pltpu.VMEM((digits, 2, lanes, 2 * lanes), jnp.float32),
        ],
        compiler_params=params(),
        cost_estimate=light(),
        name="middle",
    )(*operands)
    return [outs[p * shards:(p + 1) * shards] for p in range(len(pieces))] if pieces else outs


def space_kernel(sign, onward, keep, image, aliased, *refs):
    refs = list(refs[1:])
    me = refs.pop(0)[0]
    if image == "halves":
        bit = refs.pop(0)[0]
    scale_ref, slow_ref, itwid_ref, itable_ref = refs[:4]
    del refs[:4]
    scale = scale_ref[0]
    ins = refs[:shards]
    del refs[:shards]
    if image:
        other_ref = refs.pop(0)
    if onward:
        twid_ref, table_ref = refs[:2]
        del refs[:2]
    if aliased:
        refs.pop(0)
    field_ref = refs.pop(0) if keep else None
    if onward:
        outs = refs[:shards]
        del refs[:shards]
    if image == "halves":
        mine_ref, theirs_ref, held, image_ref = refs
    elif image:
        image_ref, held = refs
    else:
        (held,) = refs
    rows = held.shape[1]

    group = max(1, lanes // rows)
    for first in range(0, shards, group):
        wide = []
        for k in range(first, first + group):
            block = ins[k][0] if len(ins[k].shape) == 5 else ins[k][...]
            wide += [jnp.concatenate([block[j, 0], block[j, 1]], axis=1) for j in range(2)]
        done = times_right(jnp.concatenate(wide, axis=0), itable_ref)
        for n in range(group):
            part = done[2 * n * rows:2 * (n + 1) * rows]
            held[pl.ds((me ^ (first + n)) * 2, 2)] = part.reshape(2, rows, 2 * lanes)

    def one(t, carry):
        at = pl.ds(pl.multiple_of(t * sub, sub), sub)
        values = []
        for q in range(digits):
            value = (held[q, at, :lanes], held[q, at, lanes:])
            if q:
                value = product(value, (itwid_ref[0, q:q + 1, :], itwid_ref[1, q:q + 1, :]))
            values.append(value)
        values = sixteen(values, 1)
        for a in range(digits):
            real, imag = values[a]
            col = slice(a * lanes, (a + 1) * lanes)
            c, s = cos_sin(scale * slow_ref[0, at, col])
            if sign > 0:
                real, imag = real * c - imag * s, real * s + imag * c
            else:
                real, imag = real * c + imag * s, imag * c - real * s
            if keep:
                field_ref[0, at, col] = real
                field_ref[1, at, col] = imag
            if image:
                image_ref[at, col] = real * other_ref[0, at, col] + imag * other_ref[1, at, col]
            values[a] = (real, imag)
        if onward:
            for q, value in enumerate(sixteen(values, -1)):
                if q:
                    value = product(value, (twid_ref[0, q:q + 1, :], twid_ref[1, q:q + 1, :]))
                held[q, at, :lanes] = value[0]
                held[q, at, lanes:] = value[1]
        return carry

    lax.fori_loop(0, rows // sub, one, 0)
    if image == "halves":
        half = rows // 2
        mine_ref[...] = image_ref[pl.ds(pl.multiple_of(bit * half, sub), half), :]
        theirs_ref[...] = image_ref[pl.ds(pl.multiple_of((1 - bit) * half, sub), half), :]
    if onward:
        to_last_wavenumbers(me, held, table_ref, outs)


def space(me, blocks, scale, slow, store_pos, z, sign, onward, other=None, keep=True, start=0, into=None, bit=None, chunk=128, part=None, skip=0):
    _, rows, cols = slow.shape
    if isinstance(blocks, tuple):
        blocks, place = blocks
        part = part or blocks[0].shape[3]
        chunk = min(chunk, part)
        over = skip // chunk
        specs = [pl.BlockSpec((1, 2, 2, chunk, lanes), lambda i, *_: (place, 0, 0, over + i, 0))] * shards
    else:
        part = blocks[0].shape[2]
        specs = block_specs(chunk)
    first = start // chunk
    image = None if other is None else "whole" if bit is None else "halves"
    itwid, itable = twiddle_table(cols, 1), right_table(1)
    field_spec = pl.BlockSpec((2, chunk, cols), lambda i, *_: (0, first + i, 0))
    slow_spec = pl.BlockSpec((1, chunk, cols), lambda i, at: (at[z], first + i, 0))
    operands, in_specs = [store_pos, me], [smem()]
    if image == "halves":
        operands.append(bit)
        in_specs.append(smem())
    operands += [scale, slow, itwid, itable]
    in_specs += [smem(), slow_spec, whole(itwid), whole(itable)]
    operands += blocks
    in_specs += specs
    if image:
        operands.append(other)
        in_specs.append(field_spec)
    if onward:
        tables = [twiddle_table(cols, -1), right_table(-1)]
        operands += tables
        in_specs += [whole(table) for table in tables]
    aliases = {}
    if into is not None:
        aliases = {len(operands): 0}
        operands.append(into)
        in_specs.append(pl.BlockSpec(memory_space=pl.ANY))
    out_specs, out_shape = [], []
    scratch = [pltpu.VMEM((digits, chunk, 2 * lanes), jnp.float32)]
    if keep:
        out_specs.append(field_spec)
        out_shape.append(jax.ShapeDtypeStruct((2, rows, cols), jnp.float32))
    if onward:
        out_specs += block_specs(chunk)
        out_shape += block_shapes(part)
    if image == "whole":
        out_specs.append(pl.BlockSpec((chunk, cols), lambda i, *_: (i, 0)))
        out_shape.append(jax.ShapeDtypeStruct((part, cols), jnp.float32))
    elif image:
        out_specs += [pl.BlockSpec((chunk // 2, cols), lambda i, *_: (i, 0))] * 2
        out_shape += [jax.ShapeDtypeStruct((part // 2, cols), jnp.float32)] * 2
        scratch.append(pltpu.VMEM((chunk, cols), jnp.float32))
    outs = pl.pallas_call(
        functools.partial(space_kernel, sign, onward, keep, image, into is not None),
        grid_spec=pltpu.PrefetchScalarGridSpec(
            num_scalar_prefetch=1,
            grid=(part // chunk,),
            in_specs=in_specs,
            out_specs=out_specs,
            scratch_shapes=scratch,
        ),
        out_shape=out_shape,
        input_output_aliases=aliases,
        compiler_params=params(),
        cost_estimate=light(),
        name="space",
    )(*operands)
    outs = list(outs)
    field = outs.pop(0) if keep else None
    onward_blocks = outs[:shards] if onward else None
    if image == "halves":
        term = outs[-2:]
    else:
        term = outs[-1] if image else None
    return field, onward_blocks, term


def put_kernel(halved, bit_ref, *refs):
    refs, out_ref = list(refs), refs[-1]
    bit = bit_ref[0]
    at = 0
    for two in halved:
        size = refs[0].shape[0]
        if two:
            mine, theirs = refs.pop(0), refs.pop(0)
            out_ref[0, pl.ds(pl.multiple_of(at + bit * size, sub), size), :] = mine[...]
            out_ref[0, pl.ds(pl.multiple_of(at + (1 - bit) * size, sub), size), :] = theirs[...]
            at += 2 * size
        else:
            out_ref[0, at:at + size, :] = refs.pop(0)[...]
            at += size


def put(image, z, bit, sums):
    flat = []
    for value in sums:
        flat += list(value) if isinstance(value, tuple) else [value]
    in_specs = [smem()] + [whole(v) for v in flat]
    operands = [bit, *flat]
    aliases = {}
    if isinstance(image, tuple):
        shape = image
    else:
        shape = image.shape
        aliases = {len(operands): 0}
        operands.append(image)
        in_specs.append(pl.BlockSpec(memory_space=pl.ANY))
    return pl.pallas_call(
        functools.partial(put_kernel, [isinstance(value, tuple) for value in sums]),
        grid=(1,),
        in_specs=in_specs,
        out_specs=pl.BlockSpec((1,) + shape[1:], lambda i: (z, 0, 0)),
        out_shape=jax.ShapeDtypeStruct(shape, jnp.float32),
        input_output_aliases=aliases,
        compiler_params=params(),
        cost_estimate=light(),
        name="put",
    )(*operands)


def wavenumber(index, length):
    signed = jnp.where(index < length // 2, index, index - length)
    return 2.0 * jnp.pi * (signed.astype(jnp.float32) / length)


def multiplier(omega, kx_index, ky_index, rows_total, cols_total):
    kx_values = wavenumber(kx_index, rows_total)
    ky_values = wavenumber(ky_index, cols_total)
    phase_q = omega * omega - (kx_values * kx_values + ky_values * ky_values)
    travel = jnp.sqrt(jnp.maximum(phase_q, 0.0))
    decay = jnp.sqrt(jnp.maximum(-phase_q, 0.0))
    damping = jnp.exp(-depth_step * decay) / (rows_total * cols_total)
    return damping * jnp.cos(depth_step * travel), damping * jnp.sin(depth_step * travel)


def on_device(source_field, receiver_field, slowness_store, store_pos, freq_index):
    omega = omega_unit * freq_index.astype(jnp.float32)[0]
    rows = source_field.shape[2]
    cols = source_field.shape[3]
    rows_total = rows * 8
    me = lax.axis_index("row").astype(jnp.int32)[None]
    bit = lax.axis_index("freq").astype(jnp.int32)[None] & 1

    grid_shape = (digits, lanes, 2 * lanes)
    kx_index = lax.broadcasted_iota(jnp.int32, grid_shape, 0) + digits * lax.broadcasted_iota(
        jnp.int32, grid_shape, 1
    )
    column = lax.broadcasted_iota(jnp.int32, grid_shape, 2)
    ky_index = lax.axis_index("row") * 2 + column // lanes + digits * (column % lanes)
    def behind(*arrays):
        return after(me, *arrays)

    spec_source = forward_last(me, source_field[0], 128)
    moved_source = exchange(spec_source)
    slow = lax.all_gather(slowness_store, "freq", axis=0, tiled=True)
    mult = multiplier(after(omega, *moved_source), kx_index, ky_index, rows_total, cols)

    scale = (depth_step * omega)[None]

    spec_receiver = forward_last(behind(moved_source[1]), receiver_field[0], 128)
    moved_receiver = exchange(spec_receiver, moved_source)
    mid_source = middle(behind(spec_receiver[0]), moved_source, mult, -1)
    mid_receiver = middle(behind(mid_source[0]), moved_receiver, mult, 1)
    back_source = exchange(mid_source, moved_receiver)
    back_receiver = exchange(mid_receiver, back_source)
    source_now, spec_source, _ = space(behind(mid_receiver[0]), back_source, scale, slow, store_pos, 0, -1, True)
    _, spec_receiver, term = space(me, back_receiver, scale, slow, store_pos, 0, 1, True, other=source_now, keep=False)
    first_image = lax.psum(term, "freq")

    moved_source = exchange(spec_source, back_receiver)
    moved_receiver = exchange(spec_receiver, moved_source)
    sizes = (rows // 2, rows // 2)
    mid_source = middle(
        behind(spec_receiver[0]), moved_source, mult, -1,
        tuple((size, min(n, 1) + 1, 0) for n, size in enumerate(sizes)),
    )
    image = put((DEPTHS, rows, cols), 0, bit, [first_image])
    mid_receiver = middle(
        me, moved_receiver, mult, 1, tuple((size, min(n, 1) + 1, min(n, 1)) for n, size in enumerate(sizes)),
        mid_source,
    )
    late = [after(block, mid_receiver[0][0]) for block in mid_source[0][1:3]]
    first_source = exchange([mid_source[0][0], *late, *mid_source[0][3:]], moved_receiver)
    moved = exchange(mid_receiver[0], first_source)

    def finish(tie, back_source, back_receiver, start, source_now, receiver_now, part, skip):
        source_now, _, _ = space(
            tie, back_source, scale, slow, store_pos, 1, -1, False, start=start, into=source_now, part=part, skip=skip
        )
        receiver_now, _, term = space(
            me, back_receiver, scale, slow, store_pos, 1, 1, False, other=source_now, start=start,
            into=receiver_now, bit=bit, part=part, skip=skip,
        )
        return source_now, receiver_now, term

    def near_sum(term, *marks):
        mine, theirs = term
        return mine + swap(after(theirs, *marks) if marks else theirs, "freq", 1)

    def far_sum(value, *marks):
        value = after(value, *marks) if marks else value
        return value + swap(value, "freq", 2)

    half, quarter = rows // 2, rows // 4
    source_now, receiver_now, term = finish(
        behind(image), (first_source, 0), (moved, 0), 0, None, None, half, 0
    )
    blocks = mid_receiver[1]
    blocks = [blocks[0], *[after(block, term[0]) for block in blocks[1:3]], *blocks[3:]]
    moved = exchange(blocks, moved)
    pair = ((moved, 0), (moved, 1))
    near = [near_sum(term)]
    far = [far_sum(near[0])]
    source_now, receiver_now, term = finish(
        behind(near[0]), *pair, half, source_now, receiver_now, quarter, 0
    )
    back = [swap(far[0], "freq", 1)]
    near.append(near_sum(term))
    source_now, receiver_now, term = finish(
        behind(near[0]), *pair, half + quarter, source_now, receiver_now, quarter, quarter
    )
    far.append(far_sum(near[1]))
    near.append(near_sum(term, far[0], near[1]))
    far.append(far_sum(near[2], back[0]))
    back += [swap(value, "freq", 1) for value in far[1:]]
    return put(image, 1, bit, list(zip(far, back))), source_now[None], receiver_now[None]


def plain_step(field, mult_real, mult_imag):
    def table(length, orient):
        index = lax.broadcasted_iota(jnp.int32, (length, length), 0) * lax.broadcasted_iota(
            jnp.int32, (length, length), 1
        )
        angle = 2.0 * jnp.pi / length * (index % length).astype(jnp.float32)
        return jnp.cos(angle), orient * jnp.sin(angle)

    def along(real, imag, orient, last):
        c, s = table(real.shape[1 if last else 0], orient)
        dot = functools.partial(jnp.matmul, precision=lax.Precision.HIGHEST)
        if last:
            return dot(real, c) - dot(imag, s), dot(real, s) + dot(imag, c)
        return dot(c, real) - dot(s, imag), dot(s, real) + dot(c, imag)

    def trade(pair, split, join):
        both = lax.all_to_all(jnp.stack(pair), "row", split_axis=split, concat_axis=join, tiled=True)
        return both[0], both[1]

    real, imag = along(field[0], field[1], -1.0, True)
    real, imag = trade((real, imag), 2, 1)
    real, imag = along(real, imag, -1.0, False)
    real, imag = product((real, imag), (mult_real, mult_imag))
    real, imag = along(real, imag, 1.0, False)
    real, imag = trade((real, imag), 1, 2)
    return jnp.stack(along(real, imag, 1.0, True))


def on_device_plain(source_field, receiver_field, slowness_store, store_pos, freq_index):
    omega = omega_unit * freq_index.astype(jnp.float32)[0]
    rows = source_field.shape[2]
    cols = source_field.shape[3]
    shards = lax.axis_size("row")
    rows_total = rows * shards
    block = cols // shards
    slow = lax.all_gather(slowness_store, "freq", axis=0, tiled=True)
    kx_index = lax.broadcasted_iota(jnp.int32, (rows_total, block), 0)
    ky_index = lax.broadcasted_iota(jnp.int32, (rows_total, block), 1) + lax.axis_index("row") * block
    mult_real, mult_imag = multiplier(omega, kx_index, ky_index, rows_total, cols)
    source_now, receiver_now = source_field[0], receiver_field[0]
    images = []
    for z in range(DEPTHS):
        angles = depth_step * omega * slow[store_pos[z]]
        lens_cos, lens_sin = jnp.cos(angles), jnp.sin(angles)
        source_now = plain_step(source_now, mult_real, -mult_imag)
        receiver_now = plain_step(receiver_now, mult_real, mult_imag)
        source_now = jnp.stack(product(source_now, (lens_cos, -lens_sin)))
        receiver_now = jnp.stack(product(receiver_now, (lens_cos, lens_sin)))
        images.append(lax.psum(jnp.sum(source_now * receiver_now, axis=0), "freq"))
    return jnp.stack(images), source_now[None], receiver_now[None]


def solution(mesh):
    placed = (
        P("freq", None, "row", None),
        P("freq", None, "row", None),
        P("freq", "row", None),
        P(),
        P("freq"),
    )

    def chosen(source_field, *rest):
        rows, cols = source_field.shape[2:]
        split = lax.axis_size("row")
        length = digits * lanes
        fits = split == shards and lax.axis_size("freq") == 4 and cols == length and rows * split == length
        return (on_device if fits else on_device_plain)(source_field, *rest)

    return jax.shard_map(
        chosen,
        mesh=mesh,
        in_specs=placed,
        out_specs=(
            P(None, "row", None),
            P("freq", None, "row", None),
            P("freq", None, "row", None),
        ),
        check_vma=False,
    )
```
